128 devices in a mesh: grp: 4 (over z), leaf: 32 (over y, x, core).
Axes of the slice: x: 4, y: 4, z: 4, core: 2. Of those that a mesh axis runs over, the one named last changes fastest.
Arguments:
- probes: float32 [4096, 8, 256], P(('grp', 'leaf')), may hold values from -6 to 6
- coords: float32 [4096, 3, 256], P(('grp', 'leaf')), may hold values from 0 to 1
- order: int32 [4096, 256], P(('grp', 'leaf')), may hold values from 0 to 255, each once within a row
- basis: float32 [4096, 64, 256], P(('grp', 'leaf')), may hold values from -0.375 to 0.375
- transfer: float32 [4096, 4096], P(('grp', 'leaf')), may hold values from -0.25 to 0.25
- far_list: int32 [4096, 16], P(('grp', 'leaf')), may hold values from 0 to 4095, as said below
- far_count: int32 [4096], P(('grp', 'leaf')), may hold values from 8 to 16
- far_coupling: float32 [4096, 16, 4096], P(('grp', 'leaf')), may hold values from -0.25 to 0.25
- node_list: int32 [128, 8], P(('grp', 'leaf')), may hold values from 0 to 127
- node_count: int32 [128], P(('grp', 'leaf')), may hold values from 4 to 8
- node_coupling: float32 [128, 8, 4096], P(('grp', 'leaf')), may hold values from -0.75 to 0.75
- near_list: int32 [4096, 8], P(('grp', 'leaf')), may hold values from 0 to 4095, as said below
- near_count: int32 [4096], P(('grp', 'leaf')), may hold values from 4 to 8
Outputs:
- product: float32 [4096, 8, 256], P(('grp', 'leaf'))
The draws below stay inside these ranges and needn't reach their ends.
Inputs may be any that keep to these rules, and one draw needn't show every extreme that they name: `far_list`: every entry (used or not) names a leaf of the same grp subtree whose leaf block lies at most 16 blocks from the target's along leaf. `near_list`: every entry names a leaf of the same grp subtree whose leaf block is the target's or next to it along leaf.
All inputs are finite; a program needn't handle non-finite values.
Results may differ from the reference program's by a relative error of at most 0.000067.
Values sent between devices are 32-bit elements; how exact they have to be, the bound alone decides.
No kernel may reach another device: no remote copies, remote signals or barrier semaphores. Data moves between devices by JAX's collectives and lax.ppermute only.
A program may use at most 128 MiB of HBM per device.

```python
import jax
import jax.numpy as jnp
from jax import lax

LEAF = 256
RANK = 64
PROBES = 8
LEAVES_DEV = 32
KF = 16
KN = 8
KB = 8
LEAVES = 4096
NODES = 128
REACH = 16
N_LEAF = 32


def local_sources(key, slots, reach, pinned):
    leaves = jnp.arange(LEAVES, dtype=jnp.int32)
    device = leaves // LEAVES_DEV
    group = device // N_LEAF
    place = device % N_LEAF
    key_a, key_b = jax.random.split(key)
    offset = jax.random.randint(key_a, (LEAVES, slots), -reach, reach + 1)
    if pinned:
        far_step = jnp.where(place < N_LEAF // 2, N_LEAF // 2, -(N_LEAF // 2)).astype(offset.dtype)
        offset = offset.at[:, 0].set(far_step)
    moved = place[:, None] + offset
    moved = jnp.where((moved < 0) | (moved >= N_LEAF), place[:, None] - offset, moved)
    inside_group = jax.random.randint(key_b, (LEAVES, slots), 0, LEAVES_DEV)
    return ((group[:, None] * N_LEAF + moved) * LEAVES_DEV + inside_group).astype(jnp.int32)


def draw_far_list(key, part):
    key = jax.random.fold_in(key, 11)
    return local_sources(key, KF, REACH, True)


def draw_near_list(key, part):
    key = jax.random.fold_in(key, 23)
    return local_sources(key, KN, 1, False)


def plant(result, stream_key, smallest, largest):
    spot = [jax.random.randint(jax.random.fold_in(stream_key, axis), (), 0, length) for axis, length in enumerate(result.shape)]
    widest = result.shape.index(max(result.shape))
    beside = spot[:widest] + [(spot[widest] + 1) % result.shape[widest]] + spot[widest + 1:]
    return result.at[tuple(spot)].set(smallest).at[tuple(beside)].set(largest)


def levels(key, dims, cuts, smallest, high):
    loudness, own = 1.0, jax.random.fold_in(key, 6)
    for axis_at, parts in cuts:
        steps = jnp.exp(jax.random.uniform(jax.random.fold_in(own, axis_at), (parts,), jnp.float32, smallest / len(cuts), high / len(cuts)))
        loudness = loudness * jnp.repeat(steps, dims[axis_at] // parts).reshape([-1 if axis == axis_at else 1 for axis in range(len(dims))])
    return loudness


def centred(key, dims, deviation, most, cuts=(), held_as=jnp.bfloat16):
    drawn = deviation * jax.random.normal(key, dims, jnp.float32)
    if cuts:
        drawn = drawn * levels(key, dims, cuts, -0.22, 0.18)
    return jnp.clip(drawn, -most, most).astype(held_as)


def setup_inputs(seed: int = 0) -> dict:
    key_of = jax.random.split(jax.random.key(seed), 14)
    probes = centred(key_of[0], (LEAVES, PROBES, LEAF), 1.0, 6.0, ((0, 128),), jnp.float32)
    coords = jnp.clip(1.0 * jax.random.uniform(key_of[1], (LEAVES, 3, LEAF), jnp.float32) ** levels(key_of[1], (LEAVES, 3, LEAF), ((0, 128),), -0.2, 0.2), 0.0, 1.0)
    order = jax.vmap(lambda own: jax.random.permutation(own, LEAF))(jax.random.split(key_of[2], LEAVES)).reshape((LEAVES, LEAF)).astype(jnp.int32)
    basis = centred(key_of[3], (LEAVES, RANK, LEAF), LEAF ** -0.5, 0.375, ((0, 128),), jnp.float32)
    transfer = centred(key_of[4], (LEAVES, RANK * RANK), (RANK * LEAVES_DEV // 4) ** -0.5, 0.25, ((0, 128),), jnp.float32)
    far_list = draw_far_list(jax.random.fold_in(key_of[13], 71), 0)
    far_count = plant(jax.random.randint(key_of[6], (LEAVES,), KF // 2, KF + 1), jax.random.fold_in(key_of[6], 1), KF // 2, KF).astype(jnp.int32)
    far_coupling = centred(key_of[7], (LEAVES, KF, RANK * RANK), (RANK * KF // 2) ** -0.5, 0.25, ((0, 128),), jnp.float32)
    node_list = plant(jax.random.randint(key_of[8], (NODES, KB), 0, NODES), jax.random.fold_in(key_of[8], 1), 0, NODES - 1).astype(jnp.int32)
    node_count = plant(jax.random.randint(key_of[9], (NODES,), KB // 2, KB + 1), jax.random.fold_in(key_of[9], 1), KB // 2, KB).astype(jnp.int32)
    node_coupling = centred(key_of[10], (NODES, KB, RANK * RANK), RANK ** -0.5, 0.75, ((0, 128),), jnp.float32)
    near_list = draw_near_list(jax.random.fold_in(key_of[13], 71), 0)
    near_count = plant(jax.random.randint(key_of[12], (LEAVES,), KN // 2, KN + 1), jax.random.fold_in(key_of[12], 1), KN // 2, KN).astype(jnp.int32)
    return {"probes": probes, "coords": coords, "order": order, "basis": basis, "transfer": transfer, "far_list": far_list, "far_count": far_count, "far_coupling": far_coupling, "node_list": node_list, "node_count": node_count, "node_coupling": node_coupling, "near_list": near_list, "near_count": near_count}


amplitude = 0.0625
length_scale = 0.15
top_level = lax.Precision.HIGHEST

def kernel_block(target_coords, source_coords):
    dist_sq = jnp.zeros(target_coords.shape[:1] + source_coords.shape[1:2] + (target_coords.shape[-1], source_coords.shape[-1]), target_coords.dtype)
    for comp in range(3):
        diff = target_coords[:, None, comp, :, None] - source_coords[:, :, comp, None, :]
        dist_sq = dist_sq + diff * diff
    scaled = jnp.sqrt(dist_sq) * (jnp.sqrt(3.0) / length_scale)
    return amplitude * (1.0 + scaled) * jnp.exp(-scaled)

def reference(probes, coords, order, basis, transfer, far_list, far_count, far_coupling, node_list, node_count, node_coupling, near_list, near_count):
    sorted_probes = jnp.take_along_axis(probes, order[:, None, :], axis=2)
    coef = jnp.einsum('lrn,lpn->lpr', basis, sorted_probes, precision=top_level)
    transpose_flag = transfer.reshape(LEAVES, RANK, RANK)
    child = jnp.einsum('lrs,lps->lpr', transpose_flag, coef, precision=top_level)
    node_coef = child.reshape(NODES, LEAVES_DEV, PROBES, RANK).sum(axis=1)
    node_valid_mask = (jnp.arange(KB)[None, :] < node_count[:, None]).astype(coef.dtype)
    node_src = node_coef[node_list] * node_valid_mask[:, :, None, None]
    node_output = jnp.einsum('nkrs,nkps->npr', node_coupling.reshape(NODES, KB, RANK, RANK), node_src, precision=top_level)
    far_mask = (jnp.arange(KF)[None, :] < far_count[:, None]).astype(coef.dtype)
    far_src = coef[far_list] * far_mask[:, :, None, None]
    leaf_output = jnp.einsum('lkrs,lkps->lpr', far_coupling.reshape(LEAVES, KF, RANK, RANK), far_src, precision=top_level)
    node_downward = jnp.repeat(node_output, LEAVES_DEV, axis=0)
    leaf_output = leaf_output + jnp.einsum('vkt,vbk->vbt', transpose_flag, node_downward, precision=top_level)
    far_part = jnp.einsum('lrn,lpr->lpn', basis, leaf_output, precision=top_level)
    near_mask = (jnp.arange(KN)[None, :] < near_count[:, None]).astype(coef.dtype)

    def near_block(index):
        start = index * LEAVES_DEV
        tgt = lax.dynamic_slice_in_dim(coords, start, LEAVES_DEV, 0)
        lists = lax.dynamic_slice_in_dim(near_list, start, LEAVES_DEV, 0)
        mask = lax.dynamic_slice_in_dim(near_mask, start, LEAVES_DEV, 0)
        tiles = kernel_block(tgt, coords[lists]) * mask[:, :, None, None]
        return jnp.einsum('bkij,bkpj->bpi', tiles, sorted_probes[lists], precision=top_level)
    near_part = lax.map(near_block, jnp.arange(LEAVES // LEAVES_DEV)).reshape(LEAVES, PROBES, LEAF)
    total = far_part + near_part
    inverse_order = jnp.argsort(order, axis=1).astype(jnp.int32)
    return jnp.take_along_axis(total, inverse_order[:, None, :], axis=2)
```

```python
import functools
import math

import jax
import jax.numpy as jnp
from jax import lax
from jax.experimental import pallas as pl
from jax.experimental.pallas import tpu as pltpu
from jax.sharding import PartitionSpec as P

f32 = jnp.float32
bf16 = jnp.bfloat16
LOG2E = 1.0 / math.log(2.0)
AMPLITUDE = 0.0625
COORD_SCALE = math.sqrt(3.0) / 0.15 * LOG2E
LEAVES = 32
PROBES = 8
POINTS = 256
RANK = 64
UNROLL = 8
TILE_SLOTS = 264
BIG = 48 * 2**20

NT = (((1,), (1,)), ((), ()))


def split2(x):
    high = x.astype(bf16)
    return high, (x - high.astype(f32)).astype(bf16)


def pieces(x):
    high, low = split2(x)
    return jnp.concatenate([high, low], axis=0)


def fold(x):
    half = x.shape[0] // 2
    return x[:half] + x[half:]


def mm(a, b):
    return jnp.dot(a, b, preferred_element_type=f32)


def mm_nt(a, b):
    return lax.dot_general(a, b, NT, preferred_element_type=f32)


def lane_ids(shape):
    return lax.broadcasted_iota(jnp.int32, shape, len(shape) - 1)


def contract(tile, coefs, steps):
    sub = lax.broadcasted_iota(jnp.int32, (8, 128), 0)
    lane = lane_ids((8, 128))

    def over_slots(t):
        blocks = [tile(t, h) for h in range(steps)]
        vs = []
        for p in range(PROBES):
            total = blocks[0] * coefs[p][0]
            for h in range(1, steps):
                total = total + blocks[h] * coefs[p][h]
            vs.append(total)
        for dist in (1, 2, 4):
            keep = (sub & dist) == 0
            vs = [
                jnp.where(keep, a, b) + pltpu.roll(jnp.where(keep, b, a), dist, 0)
                for a, b in zip(vs[0::2], vs[1::2])
            ]
        return vs[0]

    def over_lanes(t0, bits):
        if bits == 0:
            return over_slots(t0)
        dist = 1 << (bits - 1)
        a = over_lanes(t0, bits - 1)
        b = over_lanes(t0 + dist, bits - 1)
        return jnp.where(
            (lane & dist) == 0, a + pltpu.roll(a, 128 - dist, 1), b + pltpu.roll(b, dist, 1)
        )

    y = over_lanes(0, 5)
    return y + pltpu.roll(y, 96, 1)


def lane_order():
    src = lax.broadcasted_iota(jnp.int32, (128, 128), 0)
    dst = lane_ids((128, 128))
    want = (dst & 1) * 64 + ((dst & 63) >> 1)
    return jnp.where(src == want, 1.0, 0.0).astype(bf16)


def reorder(y, perm):
    return fold(mm(pieces(y), perm))


def pack_rows(y):
    return jnp.where(lane_ids((4, 128)) < 64, y[:4], y[4:])


def unpack_rows(v):
    turned = pltpu.roll(v, 64, 1)
    low = lane_ids((4, 128)) < 64
    return jnp.concatenate([jnp.where(low, v, turned), jnp.where(low, turned, v)], axis=0)


def one_hot(order_row):
    rows = lax.broadcasted_iota(jnp.int32, (POINTS, POINTS), 0)
    return jnp.where(rows == order_row, 1.0, 0.0).astype(bf16)


def up_kernel(
    base_ref, near_list, near_count, probes, coords, order, basis, transfer,
    halo, coef, node, lists, counts, dup,
):
    base = base_ref[0]

    def leaf(l, filled):
        p16 = pieces(probes[l])
        s16 = mm(p16, one_hot(order[pl.ds(l, 1), :]))
        xyz = (coords[l] - 0.5) * COORD_SCALE
        norm = jnp.sum(xyz * xyz, axis=0, keepdims=True)
        halo[l] = jnp.concatenate([fold(s16), xyz, norm], axis=0)
        s16 = s16.astype(bf16)
        high, low = split2(basis[l])
        c = fold(
            mm_nt(s16, jnp.concatenate([high, high], 0))
            + mm_nt(s16, jnp.concatenate([low, low], 0))
        )
        dup[pl.ds(pl.multiple_of(l * 8, 8), 8), :] = c
        coef[l] = pack_rows(c)
        filled = list(filled)
        used = near_count[l]
        for k in range(8):
            row = near_list[l, k] - base
            side = lax.shift_right_logical(row, 5)
            code = l * 32 + (row & 31)
            for which in range(3):
                at = filled[which]
                lists[which, at] = code
                filled[which] = at + jnp.where((side == which) & (k < used), 1, 0)
        return tuple(filled)

    zero = jnp.int32(0)
    filled = lax.fori_loop(0, LEAVES, leaf, (zero, zero, zero), unroll=4)
    for which in range(3):
        counts[which] = filled[which]
        for pad in range(UNROLL):
            lists[which, filled[which] + pad] = LEAVES * 32

    coefs = [
        [dup[pl.ds(p + 64 * h, 8, stride=8), :] for h in range(4)] for p in range(PROBES)
    ]
    y = contract(
        lambda t, h: transfer[8 * h : 8 * h + 8, 128 * t : 128 * t + 128], coefs, 4
    )
    node[0] = pack_rows(reorder(y, lane_order()))


def near_kernel(which, lists, counts, src, own, out, feat, target, s16, acc):
    rows = lax.broadcasted_iota(jnp.int32, (4, POINTS), 0)
    unit = jnp.where(rows == 0, 1.0, 0.0)

    def prepare(l, carry):
        s16[l] = pieces(src[l, :8, :])

        def three(raw):
            high = raw.astype(bf16).astype(f32)
            rest = raw - high
            mid = rest.astype(bf16).astype(f32)
            return high, mid, rest - mid

        h, m, t = three(jnp.concatenate([src[l, 8:12, :], unit], axis=0))
        zero = jnp.zeros_like(h)
        feat[l] = jnp.concatenate([h, m, t, h, m, h, zero, zero], axis=0).T.astype(bf16)
        geo = own[l, 8:12, :]
        turned = jnp.where(rows < 3, geo * -2.0, 1.0)
        low = jnp.where(rows == 0, geo[3:4, :], 0.0)
        h, m, t = three(jnp.concatenate([turned, low], axis=0))
        target[l] = jnp.concatenate([h, h, h, m, m, t, zero, zero], axis=0).astype(bf16)
        return carry

    lax.fori_loop(0, LEAVES, prepare, 0, unroll=4)
    target[LEAVES] = jnp.zeros_like(target[LEAVES])
    acc[...] = jnp.zeros_like(acc)

    def tiles(step, carry):
        for i in range(UNROLL):
            code = lists[which, step * UNROLL + i]
            l = lax.shift_right_logical(code, 5)
            m = code & 31
            square = jnp.maximum(mm(feat[m], target[l]), 1e-30)
            dist = square * lax.rsqrt(square)
            kern = (LOG2E + dist) * jnp.exp2(-dist)
            high, low = split2(kern)
            s = s16[m]
            acc[l] += mm(s, high) + mm(s, low)
        return carry

    lax.fori_loop(0, (counts[which] + UNROLL - 1) // UNROLL, tiles, 0)
    for l in range(LEAVES):
        out[l] = fold(acc[l]) * (AMPLITUDE / LOG2E)


FAR_STEP = 4


def down_kernel(
    far_rows, node_rows, coupling, table_a, table_b, node_coupling, transfer, basis, order, near_a,
    near_b, near_c, out, table, picked, y_all, from_node,
):
    step = pl.program_id(0)
    count = table_a.shape[0]

    def pick(row, k):
        picked[pl.ds(k * 8, 8), :] = unpack_rows(table[row])

    @pl.when(step == 0)
    def _():
        table[:count] = table_a[...]
        table[count : 2 * count] = table_b[...]
        table[2 * count] = jnp.zeros((4, 128), f32)
        for k in range(8):
            pick(node_rows[k], k)
        coefs = [[picked[pl.ds(p, 8, stride=8), :]] for p in range(PROBES)]
        y = contract(lambda t, h: node_coupling[0, :, 128 * t : 128 * t + 128], coefs, 1)
        low = lane_ids((8, 128)) < 64
        wide = [
            jnp.where(low, y[:, t : t + 1], y[:, 64 + t : 65 + t]) for t in range(32)
        ]
        for h in range(4):
            blocks = [transfer[8 * h : 8 * h + 8, 128 * t : 128 * t + 128] for t in range(32)]
            for p in range(PROBES):
                total = blocks[0] * wide[0][p : p + 1, :]
                for t in range(1, 32):
                    total = total + blocks[t] * wide[t][p : p + 1, :]
                from_node[pl.ds(p + 64 * h, 8, stride=8), :] = total + pltpu.roll(total, 64, 1)

    for i in range(FAR_STEP):
        l = step * FAR_STEP + i
        for k in range(16):
            picked[pl.ds(128 * i + k * 8, 8), :] = unpack_rows(table[far_rows[l, k]])
        coefs = [
            [picked[pl.ds(128 * i + p + 64 * h, 8, stride=8), :] for h in range(2)]
            for p in range(PROBES)
        ]
        y_all[l] = contract(
            lambda t, h: coupling[i, 8 * h : 8 * h + 8, 128 * t : 128 * t + 128], coefs, 2
        )

    @pl.when(step == LEAVES // FAR_STEP - 1)
    def _():
        perm = lane_order()

        def leaf(l, carry):
            near = near_a[l] + near_b[l] + near_c[l]
            leaf_out = (
                reorder(y_all[l], perm) + from_node[pl.ds(pl.multiple_of(l * 8, 8), 8), :]
            )[:, :RANK]
            high, low = split2(basis[l])
            leaf16 = pieces(leaf_out)
            total = fold(mm(leaf16, high) + mm(leaf16, low)) + near
            out[l] = fold(mm_nt(pieces(total), one_hot(order[pl.ds(l, 1), :])))
            return carry

        lax.fori_loop(0, LEAVES, leaf, 0, unroll=8)


VM = pl.BlockSpec(memory_space=pltpu.VMEM)
SM = pl.BlockSpec(memory_space=pltpu.SMEM)


def near_call(which, lists, counts, src, own):
    return pl.pallas_call(
        functools.partial(near_kernel, which),
        out_shape=jax.ShapeDtypeStruct((LEAVES, PROBES, POINTS), f32),
        in_specs=[SM, SM, VM, VM],
        out_specs=VM,
        scratch_shapes=[
            pltpu.VMEM((LEAVES, POINTS, 64), bf16),
            pltpu.VMEM((LEAVES + 1, 64, POINTS), bf16),
            pltpu.VMEM((LEAVES, 16, POINTS), bf16),
            pltpu.VMEM((LEAVES + 1, 16, POINTS), f32),
        ],
        compiler_params=pltpu.CompilerParams(vmem_limit_bytes=BIG),
        cost_estimate=pl.CostEstimate(
            flops=4 * 10**9, bytes_accessed=10**6, transcendentals=8 * 10**6
        ),
        name=f"near_{which}",
    )(lists, counts, src, own)


def body(
    probes, coords, order, basis, transfer, far_list, far_count, far_coupling, node_list,
    node_count, node_coupling, near_list, near_count,
):
    grp, leaf = lax.axis_index("grp"), lax.axis_index("leaf")
    groups, blocks = lax.axis_size("grp"), lax.axis_size("leaf")
    device = grp * blocks + leaf
    base = ((device - 1) * LEAVES).reshape(1).astype(jnp.int32)

    halo, coef, node, lists, counts = pl.pallas_call(
        up_kernel,
        out_shape=(
            jax.ShapeDtypeStruct((LEAVES, 12, POINTS), f32),
            jax.ShapeDtypeStruct((LEAVES, 4, 128), f32),
            jax.ShapeDtypeStruct((1, 4, 128), f32),
            jax.ShapeDtypeStruct((3, TILE_SLOTS), jnp.int32),
            jax.ShapeDtypeStruct((3,), jnp.int32),
        ),
        in_specs=[SM, SM, SM, VM, VM, VM, VM, VM],
        out_specs=(VM, VM, VM, SM, SM),
        scratch_shapes=[pltpu.VMEM((LEAVES * 8, 128), f32)],
        compiler_params=pltpu.CompilerParams(vmem_limit_bytes=BIG),
        name="up",
    )(base, near_list, near_count, probes, coords, order, basis, transfer)

    ahead = [(i, i + 1) for i in range(blocks - 1)]
    behind = [(i + 1, i) for i in range(blocks - 1)]
    below = lax.ppermute(halo, "leaf", ahead)
    above = lax.ppermute(halo, "leaf", behind)

    nodes = [node] + [
        lax.ppermute(node, "grp", [((g + i) % groups, g) for g in range(groups)])
        for i in range(1, groups)
    ]
    part = jnp.concatenate([coef] + nodes, axis=0)

    def place(y, x, c):
        return ((y % 4) * 4 + x % 4) * 2 + c

    everyone = [(y, x, c) for y in range(4) for x in range(4) for c in range(2)]
    part = jnp.concatenate(
        [part]
        + [
            lax.ppermute(part, "leaf", [(place(y, x + i, c), place(y, x, c)) for y, x, c in everyone])
            for i in range(1, 4)
        ],
        axis=0,
    )
    part = jnp.concatenate(
        [part]
        + [
            lax.ppermute(part, "leaf", [(place(y + i, x, c), place(y, x, c)) for y, x, c in everyone])
            for i in range(1, 4)
        ],
        axis=0,
    )
    other = lax.ppermute(
        part, "leaf", [(place(y, x, 1 - c), place(y, x, c)) for y, x, c in everyone]
    )
    held = LEAVES + groups
    empty = 32 * held

    def slot_of(block):
        y, x, c = block // 8, (block // 2) % 4, block % 2
        my_y, my_x, my_c = leaf // 8, (leaf // 2) % 4, leaf % 2
        return ((c != my_c) * 16 + ((y - my_y) % 4) * 4 + (x - my_x) % 4) * held

    local = far_list - grp * blocks * LEAVES
    far_rows = jnp.where(
        jnp.arange(far_list.shape[1])[None, :] < far_count[:, None],
        slot_of(local // LEAVES) + local % LEAVES,
        empty,
    ).astype(jnp.int32)
    node_rows = jnp.where(
        jnp.arange(node_list.shape[1]) < node_count[0],
        slot_of(node_list[0] % blocks) + LEAVES + (node_list[0] // blocks - grp) % groups,
        empty,
    ).astype(jnp.int32)

    near = [
        near_call(1, lists, counts, halo, halo),
        near_call(0, lists, counts, below, halo),
        near_call(2, lists, counts, above, halo),
    ]

    whole = lambda *shape: pl.BlockSpec(shape, lambda i: (0,) * len(shape))
    out = pl.pallas_call(
        down_kernel,
        grid=(LEAVES // FAR_STEP,),
        out_shape=jax.ShapeDtypeStruct((LEAVES, PROBES, POINTS), f32),
        in_specs=[SM, SM, pl.BlockSpec((FAR_STEP, 16, RANK * RANK), lambda i: (i, 0, 0))] + [VM] * 9,
        out_specs=VM,
        scratch_shapes=[
            pltpu.VMEM((empty + 1, 4, 128), f32),
            pltpu.VMEM((FAR_STEP * 128, 128), f32),
            pltpu.VMEM((LEAVES, 8, 128), f32),
            pltpu.VMEM((LEAVES * 8, 128), f32),
        ],
        compiler_params=pltpu.CompilerParams(vmem_limit_bytes=BIG),
        name="down",
    )(far_rows, node_rows, far_coupling, part, other, node_coupling, transfer, basis, order, *near)
    return out


def solution(mesh):
    rows = ("grp", "leaf")
    return jax.shard_map(
        body,
        mesh=mesh,
        in_specs=(
            P(rows, None, None), P(rows, None, None), P(rows, None), P(rows, None, None),
            P(rows, None), P(rows, None), P(rows), P(rows, None, None), P(rows, None), P(rows),
            P(rows, None, None), P(rows, None), P(rows),
        ),
        out_specs=P(rows, None, None),
        check_vma=False,
    )
```

```python
import functools
import math

import jax
import jax.numpy as jnp
from jax import lax
from jax.experimental import pallas as pl
from jax.experimental.pallas import tpu as pltpu
from jax.sharding import PartitionSpec as P

f32 = jnp.float32
bf16 = jnp.bfloat16
LOG2E = 1.0 / math.log(2.0)
AMPLITUDE = 0.0625
COORD_SCALE = math.sqrt(3.0) / 0.15 * LOG2E
LEAVES = 32
PROBES = 8
POINTS = 256
RANK = 64
UNROLL = 8
TILE_SLOTS = 264
BIG = 48 * 2**20

NT = (((1,), (1,)), ((), ()))


def split2(x):
    high = x.astype(bf16)
    return high, (x - high.astype(f32)).astype(bf16)


def pieces(x):
    high, low = split2(x)
    return jnp.concatenate([high, low], axis=0)


def fold(x):
    half = x.shape[0] // 2
    return x[:half] + x[half:]


def mm(a, b):
    return jnp.dot(a, b, preferred_element_type=f32)


def mm_nt(a, b):
    return lax.dot_general(a, b, NT, preferred_element_type=f32)


def lane_ids(shape):
    return lax.broadcasted_iota(jnp.int32, shape, len(shape) - 1)


def contract(tile, coefs, steps):
    sub = lax.broadcasted_iota(jnp.int32, (8, 128), 0)
    lane = lane_ids((8, 128))

    def over_slots(t):
        blocks = [tile(t, h) for h in range(steps)]
        vs = []
        for p in range(PROBES):
            total = blocks[0] * coefs[p][0]
            for h in range(1, steps):
                total = total + blocks[h] * coefs[p][h]
            vs.append(total)
        for dist in (1, 2, 4):
            keep = (sub & dist) == 0
            vs = [
                jnp.where(keep, a, b) + pltpu.roll(jnp.where(keep, b, a), dist, 0)
                for a, b in zip(vs[0::2], vs[1::2])
            ]
        return vs[0]

    def over_lanes(t0, bits):
        if bits == 0:
            return over_slots(t0)
        dist = 1 << (bits - 1)
        a = over_lanes(t0, bits - 1)
        b = over_lanes(t0 + dist, bits - 1)
        return jnp.where(
            (lane & dist) == 0, a + pltpu.roll(a, 128 - dist, 1), b + pltpu.roll(b, dist, 1)
        )

    y = over_lanes(0, 5)
    return y + pltpu.roll(y, 96, 1)


def lane_order():
    src = lax.broadcasted_iota(jnp.int32, (128, 128), 0)
    dst = lane_ids((128, 128))
    want = (dst & 1) * 64 + ((dst & 63) >> 1)
    return jnp.where(src == want, 1.0, 0.0).astype(bf16)


def reorder(y, perm):
    return fold(mm(pieces(y), perm))


def pack_rows(y):
    return jnp.where(lane_ids((4, 128)) < 64, y[:4], y[4:])


def unpack_rows(v):
    turned = pltpu.roll(v, 64, 1)
    low = lane_ids((4, 128)) < 64
    return jnp.concatenate([jnp.where(low, v, turned), jnp.where(low, turned, v)], axis=0)


def one_hot(order_row):
    rows = lax.broadcasted_iota(jnp.int32, (POINTS, POINTS), 0)
    return jnp.where(rows == order_row, 1.0, 0.0).astype(bf16)


UP_STEP = 8


def up_kernel(
    base_ref, near_list, near_count, probes, coords, order, basis, transfer_hbm,
    halo, coef, lists, counts, dup, transfer, sem,
):
    step = pl.program_id(0)
    fetch = pltpu.make_async_copy(transfer_hbm, transfer, sem)

    @pl.when(step == 0)
    def _():
        fetch.start()
        for which in range(3):
            counts[which] = 0

    base, lowest, highest = base_ref[0], base_ref[1], base_ref[2]

    def leaf(i, filled):
        l = step * UP_STEP + i
        p16 = pieces(probes[i])
        s16 = mm(p16, one_hot(order[pl.ds(i, 1), :]))
        xyz = (coords[i] - 0.5) * COORD_SCALE
        norm = jnp.sum(xyz * xyz, axis=0, keepdims=True)
        halo[l] = jnp.concatenate([fold(s16), xyz, norm], axis=0)
        s16 = s16.astype(bf16)
        high, low = split2(basis[i])
        c = fold(
            mm_nt(s16, jnp.concatenate([high, high], 0))
            + mm_nt(s16, jnp.concatenate([low, low], 0))
        )
        dup[pl.ds(pl.multiple_of(l * 8, 8), 8), :] = c
        coef[l] = pack_rows(c)
        filled = list(filled)
        used = near_count[l]
        for k in range(8):
            row = near_list[l, k] - base
            side = lax.shift_right_logical(row, 5)
            if k % 2 == 0:
                side = jnp.where((lowest == 1) & (side == 2), 0, side)
            else:
                side = jnp.where((highest == 1) & (side == 0), 2, side)
            code = l * 32 + (row & 31)
            for which in range(3):
                at = filled[which]
                lists[which, at] = code
                filled[which] = at + jnp.where((side == which) & (k < used), 1, 0)
        return tuple(filled)

    filled = tuple(counts[which] for which in range(3))
    filled = lax.fori_loop(0, UP_STEP, leaf, filled, unroll=4)
    for which in range(3):
        counts[which] = filled[which]

    @pl.when(step == LEAVES // UP_STEP - 1)
    def _():
        for which in range(3):
            for pad in range(UNROLL):
                lists[which, filled[which] + pad] = LEAVES * 32
        fetch.wait()
        coefs = [
            [dup[pl.ds(p + 64 * h, 8, stride=8), :] for h in range(4)] for p in range(PROBES)
        ]
        y = contract(
            lambda t, h: transfer[8 * h : 8 * h + 8, 128 * t : 128 * t + 128], coefs, 4
        )
        coef[LEAVES] = pack_rows(reorder(y, lane_order()))


def near_kernel(
    which, edge, lists, counts, low_src, high_src, own, after, out, feat, target, s16, acc, src, sem
):
    del after
    for first in (True, False):
        @pl.when((edge[0] == 0) == first)
        def _():
            copy = pltpu.make_async_copy(low_src if first else high_src, src, sem)
            copy.start()
            copy.wait()

    rows = lax.broadcasted_iota(jnp.int32, (4, POINTS), 0)
    unit = jnp.where(rows == 0, 1.0, 0.0)

    def prepare(l, carry):
        s16[l] = pieces(src[l, :8, :])

        def three(raw):
            high = raw.astype(bf16).astype(f32)
            rest = raw - high
            mid = rest.astype(bf16).astype(f32)
            return high, mid, rest - mid

        h, m, t = three(jnp.concatenate([src[l, 8:12, :], unit], axis=0))
        zero = jnp.zeros_like(h)
        feat[l] = jnp.concatenate([h, m, t, h, m, h, zero, zero], axis=0).T.astype(bf16)
        geo = own[l, 8:12, :]
        turned = jnp.where(rows < 3, geo * -2.0, 1.0)
        low = jnp.where(rows == 0, geo[3:4, :], 0.0)
        h, m, t = three(jnp.concatenate([turned, low], axis=0))
        target[l] = jnp.concatenate([h, h, h, m, m, t, zero, zero], axis=0).astype(bf16)
        return carry

    lax.fori_loop(0, LEAVES, prepare, 0, unroll=4)
    target[LEAVES] = jnp.zeros_like(target[LEAVES])
    acc[...] = jnp.zeros_like(acc)

    def tiles(step, carry):
        for i in range(UNROLL):
            code = lists[which, step * UNROLL + i]
            l = lax.shift_right_logical(code, 5)
            m = code & 31
            square = jnp.maximum(mm(feat[m], target[l]), 1e-30)
            dist = square * lax.rsqrt(square)
            kern = (LOG2E + dist) * jnp.exp2(-dist)
            high, low = split2(kern)
            s = s16[m]
            acc[l] += mm(s, high) + mm(s, low)
        return carry

    lax.fori_loop(0, (counts[which] + UNROLL - 1) // UNROLL, tiles, 0)
    for l in range(LEAVES):
        out[l] = fold(acc[l]) * (AMPLITUDE / LOG2E)


def join_kernel(*refs):
    parts, after, out, sems = refs[:4], refs[4], refs[5], refs[6]
    del after
    size = parts[0].shape[0]
    copies = [
        pltpu.make_async_copy(part, out.at[pl.ds(i * size, size)], sems.at[i])
        for i, part in enumerate(parts)
    ]
    for copy in copies:
        copy.start()
    for copy in copies:
        copy.wait()


def nodes_kernel(*refs):
    parts, after, out, sem = refs[:8], refs[8], refs[9], refs[10]
    del after
    copies = [
        pltpu.make_async_copy(
            part.at[pl.ds(j * HELD + LEAVES, 1)], out.at[pl.ds(4 * i + j, 1)], sem.at[4 * i + j]
        )
        for i, part in enumerate(parts)
        for j in range(4)
    ]
    for copy in copies:
        copy.start()
    for copy in copies:
        copy.wait()


FAR_STEP = 4
HELD = LEAVES + 1
EMPTY = 32 * HELD


def far_kernel(*refs):
    far_rows, coupling, parts, after = refs[0], refs[1], refs[2:10], refs[10]
    out, table, picked, sems = refs[11:]
    del after
    step = pl.program_id(0)

    @pl.when(step == 0)
    def _():
        size = parts[0].shape[0]
        copies = [
            pltpu.make_async_copy(part, table.at[pl.ds(i * size, size)], sems.at[i])
            for i, part in enumerate(parts)
        ]
        for copy in copies:
            copy.start()
        table[EMPTY] = jnp.zeros((4, 128), f32)
        for copy in copies:
            copy.wait()

    for i in range(FAR_STEP):
        l = step * FAR_STEP + i
        for k in range(16):
            picked[pl.ds(128 * i + k * 8, 8), :] = unpack_rows(table[far_rows[l, k]])
        coefs = [
            [picked[pl.ds(128 * i + p + 64 * h, 8, stride=8), :] for h in range(2)]
            for p in range(PROBES)
        ]
        out[l] = contract(
            lambda t, h: coupling[i, 8 * h : 8 * h + 8, 128 * t : 128 * t + 128], coefs, 2
        )


def down_kernel(
    node_rows, nodes0, nodes1, nodes2, nodes3, node_coupling, transfer, basis, order, far,
    near_a, near_b, near_c, out, table, picked, wide, from_node,
):
    for g, nodes in enumerate((nodes0, nodes1, nodes2, nodes3)):
        table[32 * g : 32 * g + 32] = nodes[...]
    table[128] = jnp.zeros((4, 128), f32)
    for k in range(8):
        picked[pl.ds(k * 8, 8), :] = unpack_rows(table[node_rows[k]])
    coefs = [[picked[pl.ds(p, 8, stride=8), :]] for p in range(PROBES)]
    y = contract(lambda t, h: node_coupling[0, :, 128 * t : 128 * t + 128], coefs, 1)
    low = lane_ids((8, 128)) < 64
    for t in range(32):
        wide[:, 128 * t : 128 * t + 128] = jnp.where(low, y[:, t : t + 1], y[:, 64 + t : 65 + t])
    for p in range(PROBES):
        totals = [jnp.zeros((8, 128), f32)] * 4
        for t in range(32):
            factor = wide[p : p + 1, 128 * t : 128 * t + 128]
            for h in range(4):
                totals[h] += transfer[8 * h : 8 * h + 8, 128 * t : 128 * t + 128] * factor
        for h in range(4):
            from_node[pl.ds(p + 64 * h, 8, stride=8), :] = totals[h] + pltpu.roll(totals[h], 64, 1)

    perm = lane_order()

    def leaf(l, carry):
        near = near_a[l] + near_b[l] + near_c[l]
        leaf_out = (
            reorder(far[l], perm) + from_node[pl.ds(pl.multiple_of(l * 8, 8), 8), :]
        )[:, :RANK]
        high, lower = split2(basis[l])
        leaf16 = pieces(leaf_out)
        total = fold(mm(leaf16, high) + mm(leaf16, lower)) + near
        out[l] = fold(mm_nt(pieces(total), one_hot(order[pl.ds(l, 1), :])))
        return carry

    lax.fori_loop(0, LEAVES, leaf, 0, unroll=8)


VM = pl.BlockSpec(memory_space=pltpu.VMEM)
SM = pl.BlockSpec(memory_space=pltpu.SMEM)
ANY = pl.BlockSpec(memory_space=pl.ANY)


def near_call(which, edge, lists, counts, low_src, high_src, own, after):
    return pl.pallas_call(
        functools.partial(near_kernel, which),
        out_shape=jax.ShapeDtypeStruct((LEAVES, PROBES, POINTS), f32),
        in_specs=[SM, SM, SM, ANY, ANY, VM, ANY],
        out_specs=VM,
        scratch_shapes=[
            pltpu.VMEM((LEAVES, POINTS, 64), bf16),
            pltpu.VMEM((LEAVES + 1, 64, POINTS), bf16),
            pltpu.VMEM((LEAVES, 16, POINTS), bf16),
            pltpu.VMEM((LEAVES + 1, 16, POINTS), f32),
            pltpu.VMEM((LEAVES, 12, POINTS), f32),
            pltpu.SemaphoreType.DMA,
        ],
        compiler_params=pltpu.CompilerParams(vmem_limit_bytes=BIG),
        cost_estimate=pl.CostEstimate(
            flops=12 * 10**9, bytes_accessed=30 * 10**6, transcendentals=8 * 10**6
        ),
        name=f"near_{which}",
    )(edge, lists, counts, low_src, high_src, own, after)


def body(
    probes, coords, order, basis, transfer, far_list, far_count, far_coupling, node_list,
    node_count, node_coupling, near_list, near_count,
):
    grp, leaf = lax.axis_index("grp"), lax.axis_index("leaf")
    groups, blocks = lax.axis_size("grp"), lax.axis_size("leaf")
    device = grp * blocks + leaf
    lowest, highest = leaf == 0, leaf == blocks - 1
    base = jnp.stack([(device - 1) * LEAVES, lowest, highest]).astype(jnp.int32)
    some = lambda *shape: jax.ShapeDtypeStruct(shape, f32)
    ints = lambda *shape: jax.ShapeDtypeStruct(shape, jnp.int32)

    rows = lambda *shape: pl.BlockSpec((UP_STEP,) + shape, lambda i: (i,) + (0,) * len(shape))
    halo, coef, lists, counts = pl.pallas_call(
        up_kernel,
        grid=(LEAVES // UP_STEP,),
        out_shape=(
            some(LEAVES, 12, POINTS), some(HELD, 4, 128), ints(3, TILE_SLOTS), ints(3),
        ),
        in_specs=[SM, SM, SM, rows(8, POINTS), rows(3, POINTS), rows(POINTS), rows(RANK, POINTS), ANY],
        out_specs=(VM, VM, SM, SM),
        scratch_shapes=[
            pltpu.VMEM((LEAVES * 8, 128), f32),
            pltpu.VMEM((LEAVES, RANK * RANK), f32),
            pltpu.SemaphoreType.DMA,
        ],
        compiler_params=pltpu.CompilerParams(vmem_limit_bytes=60 * 2**20),
        name="up",
    )(base, near_list, near_count, probes, coords, order, basis, transfer)

    below = lax.ppermute(halo, "leaf", [(i, i + 1) for i in range(blocks - 1)])
    above = lax.ppermute(halo, "leaf", [(i + 1, i) for i in range(blocks - 1)])

    def place(y, x, c):
        return ((y % 4) * 4 + x % 4) * 2 + c

    everyone = [(y, x, c) for y in range(4) for x in range(4) for c in range(2)]

    def shift(part, dy, dx, dc):
        pairs = [(place(y + dy, x + dx, c ^ dc), place(y, x, c)) for y, x, c in everyone]
        return lax.ppermute(part, "leaf", pairs)

    along_x = [coef] + [shift(coef, 0, i, 0) for i in range(1, 4)]
    own_side = jnp.zeros((1,), jnp.int32)
    near_a = near_call(1, own_side, lists, counts, halo, halo, halo, coef)
    line = pl.pallas_call(
        join_kernel,
        out_shape=some(4 * HELD, 4, 128),
        in_specs=[ANY] * 5,
        out_specs=ANY,
        scratch_shapes=[pltpu.SemaphoreType.DMA((4,))],
        name="join",
    )(*along_x, near_a)
    planes = [line] + [shift(line, i, 0, 0) for i in range(1, 4)]
    near_b = near_call(
        0, lowest.astype(jnp.int32).reshape(1), lists, counts, below, above, halo, line
    )
    planes = planes + [shift(plane, 0, 0, 1) for plane in planes]
    near_c = near_call(
        2, (1 - highest.astype(jnp.int32)).reshape(1), lists, counts, below, above, halo, near_b
    )
    nodes = pl.pallas_call(
        nodes_kernel,
        out_shape=some(blocks, 4, 128),
        in_specs=[ANY] * 9,
        out_specs=ANY,
        scratch_shapes=[pltpu.SemaphoreType.DMA((32,))],
        name="nodes",
    )(*planes, near_c)
    all_nodes = [nodes] + [
        lax.ppermute(nodes, "grp", [((g + i) % groups, g) for g in range(groups)])
        for i in range(1, groups)
    ]

    def slot_of(block):
        y, x, c = block // 8, (block // 2) % 4, block % 2
        my_y, my_x, my_c = leaf // 8, (leaf // 2) % 4, leaf % 2
        return (c ^ my_c) * 16 + ((y - my_y) % 4) * 4 + (x - my_x) % 4

    local = far_list - grp * blocks * LEAVES
    far_rows = jnp.where(
        jnp.arange(far_list.shape[1])[None, :] < far_count[:, None],
        slot_of(local // LEAVES) * HELD + local % LEAVES,
        EMPTY,
    ).astype(jnp.int32)
    node_rows = jnp.where(
        jnp.arange(node_list.shape[1]) < node_count[0],
        (node_list[0] // blocks - grp) % groups * blocks + slot_of(node_list[0] % blocks),
        groups * blocks,
    ).astype(jnp.int32)

    far = pl.pallas_call(
        far_kernel,
        grid=(LEAVES // FAR_STEP,),
        out_shape=some(LEAVES, 8, 128),
        in_specs=[SM, pl.BlockSpec((FAR_STEP, 16, RANK * RANK), lambda i: (i, 0, 0))] + [ANY] * 9,
        out_specs=VM,
        scratch_shapes=[
            pltpu.VMEM((EMPTY + 1, 4, 128), f32),
            pltpu.VMEM((FAR_STEP * 128, 128), f32),
            pltpu.SemaphoreType.DMA((8,)),
        ],
        compiler_params=pltpu.CompilerParams(vmem_limit_bytes=BIG),
        cost_estimate=pl.CostEstimate(
            flops=12 * 10**9, bytes_accessed=20 * 10**6, transcendentals=0
        ),
        name="far",
    )(far_rows, far_coupling, *planes, nodes)

    return pl.pallas_call(
        down_kernel,
        out_shape=some(LEAVES, PROBES, POINTS),
        in_specs=[SM] + [VM] * 12,
        out_specs=VM,
        scratch_shapes=[
            pltpu.VMEM((129, 4, 128), f32),
            pltpu.VMEM((64, 128), f32),
            pltpu.VMEM((8, RANK * RANK), f32),
            pltpu.VMEM((LEAVES * 8, 128), f32),
        ],
        compiler_params=pltpu.CompilerParams(vmem_limit_bytes=BIG),
        name="down",
    )(
        node_rows, *all_nodes, node_coupling, transfer, basis, order, far, near_a, near_b, near_c
    )


def solution(mesh):
    rows = ("grp", "leaf")
    return jax.shard_map(
        body,
        mesh=mesh,
        in_specs=(
            P(rows, None, None), P(rows, None, None), P(rows, None), P(rows, None, None),
            P(rows, None), P(rows, None), P(rows), P(rows, None, None), P(rows, None), P(rows),
            P(rows, None, None), P(rows, None), P(rows),
        ),
        out_specs=P(rows, None, None),
        check_vma=False,
    )
```

```python
import functools
import math

import jax
import jax.numpy as jnp
from jax import lax
from jax.experimental import pallas as pl
from jax.experimental.pallas import tpu as pltpu
from jax.sharding import PartitionSpec as P

f32 = jnp.float32
bf16 = jnp.bfloat16
LOG2E = 1.0 / math.log(2.0)
AMPLITUDE = 0.0625
COORD_SCALE = math.sqrt(3.0) / 0.15 * LOG2E
LEAVES = 32
PROBES = 8
POINTS = 256
RANK = 64
UNROLL = 8
TILE_SLOTS = 264
BIG = 20 * 2**20

NT = (((1,), (1,)), ((), ()))


def split2(x):
    high = x.astype(bf16)
    return high, (x - high.astype(f32)).astype(bf16)


def pieces(x):
    high, low = split2(x)
    return jnp.concatenate([high, low], axis=0)


def fold(x):
    half = x.shape[0] // 2
    return x[:half] + x[half:]


def mm(a, b):
    return jnp.dot(a, b, preferred_element_type=f32)


def mm_nt(a, b):
    return lax.dot_general(a, b, NT, preferred_element_type=f32)


def lane_ids(shape):
    return lax.broadcasted_iota(jnp.int32, shape, len(shape) - 1)


def contract(tile, coefs, steps):
    sub = lax.broadcasted_iota(jnp.int32, (8, 128), 0)
    lane = lane_ids((8, 128))

    def over_slots(t):
        blocks = [tile(t, h) for h in range(steps)]
        vs = []
        for p in range(PROBES):
            total = blocks[0] * coefs[p][0]
            for h in range(1, steps):
                total = total + blocks[h] * coefs[p][h]
            vs.append(total)
        for dist in (1, 2, 4):
            keep = (sub & dist) == 0
            vs = [
                jnp.where(keep, a, b) + pltpu.roll(jnp.where(keep, b, a), dist, 0)
                for a, b in zip(vs[0::2], vs[1::2])
            ]
        return vs[0]

    def over_lanes(t0, bits):
        if bits == 0:
            return over_slots(t0)
        dist = 1 << (bits - 1)
        a = over_lanes(t0, bits - 1)
        b = over_lanes(t0 + dist, bits - 1)
        return jnp.where(
            (lane & dist) == 0, a + pltpu.roll(a, 128 - dist, 1), b + pltpu.roll(b, dist, 1)
        )

    y = over_lanes(0, 5)
    return y + pltpu.roll(y, 96, 1)


def lane_order():
    src = lax.broadcasted_iota(jnp.int32, (128, 128), 0)
    dst = lane_ids((128, 128))
    want = (dst & 1) * 64 + ((dst & 63) >> 1)
    return jnp.where(src == want, 1.0, 0.0).astype(bf16)


def reorder(y, perm):
    return fold(mm(pieces(y), perm))


def pack_rows(y):
    return jnp.where(lane_ids((4, 128)) < 64, y[:4], y[4:])


def unpack_rows(v):
    turned = pltpu.roll(v, 64, 1)
    low = lane_ids((4, 128)) < 64
    return jnp.concatenate([jnp.where(low, v, turned), jnp.where(low, turned, v)], axis=0)


def one_hot(order_row):
    rows = lax.broadcasted_iota(jnp.int32, (POINTS, POINTS), 0)
    return jnp.where(rows == order_row, 1.0, 0.0).astype(bf16)


UP_STEP = 8


def up_kernel(
    base_ref, near_list, near_count, probes, coords, order, basis, transfer_hbm,
    halo, coef, lists, counts, dup, transfer, sem,
):
    step = pl.program_id(0)
    fetch = pltpu.make_async_copy(transfer_hbm, transfer, sem)

    @pl.when(step == 0)
    def _():
        fetch.start()
        for which in range(3):
            counts[which] = 0

    base, lowest, highest = base_ref[0], base_ref[1], base_ref[2]

    def leaf(i, filled):
        l = step * UP_STEP + i
        p16 = pieces(probes[i])
        s16 = mm(p16, one_hot(order[pl.ds(i, 1), :]))
        xyz = jnp.concatenate([coords[c, pl.ds(i, 1), :] for c in range(3)], axis=0)
        xyz = (xyz - 0.5) * COORD_SCALE
        norm = jnp.sum(xyz * xyz, axis=0, keepdims=True)
        halo[l] = jnp.concatenate([fold(s16), xyz, norm], axis=0)
        s16 = s16.astype(bf16)
        high, low = split2(basis[i])
        c = fold(
            mm_nt(s16, jnp.concatenate([high, high], 0))
            + mm_nt(s16, jnp.concatenate([low, low], 0))
        )
        dup[pl.ds(pl.multiple_of(l * 8, 8), 8), :] = c
        coef[l] = pack_rows(c)
        filled = list(filled)
        used = near_count[l]
        for k in range(8):
            row = near_list[k, l] - base
            side = lax.shift_right_logical(row, 5)
            if k % 2 == 0:
                side = jnp.where((lowest == 1) & (side == 2), 0, side)
            else:
                side = jnp.where((highest == 1) & (side == 0), 2, side)
            code = l * 32 + (row & 31)
            for which in range(3):
                at = filled[which]
                lists[which, at] = code
                filled[which] = at + jnp.where((side == which) & (k < used), 1, 0)
        return tuple(filled)

    filled = tuple(counts[which] for which in range(3))
    filled = lax.fori_loop(0, UP_STEP, leaf, filled, unroll=4)
    for which in range(3):
        counts[which] = filled[which]

    @pl.when(step == LEAVES // UP_STEP - 1)
    def _():
        for which in range(3):
            for pad in range(UNROLL):
                lists[which, filled[which] + pad] = LEAVES * 32
        fetch.wait()
        coefs = [
            [dup[pl.ds(p + 64 * h, 8, stride=8), :] for h in range(4)] for p in range(PROBES)
        ]
        y = contract(
            lambda t, h: transfer[8 * h : 8 * h + 8, 128 * t : 128 * t + 128], coefs, 4
        )
        coef[LEAVES] = pack_rows(reorder(y, lane_order()))


def near_kernel(
    which, edge, lists, counts, low_src, high_src, own, out, feat, target, s16, acc, src, sem
):
    for first in (True, False):
        @pl.when((edge[0] == 0) == first)
        def _():
            copy = pltpu.make_async_copy(low_src if first else high_src, src, sem)
            copy.start()
            copy.wait()

    rows = lax.broadcasted_iota(jnp.int32, (4, POINTS), 0)
    unit = jnp.where(rows == 0, 1.0, 0.0)

    def prepare(l, carry):
        s16[l] = pieces(src[l, :8, :])

        def three(raw):
            high = raw.astype(bf16).astype(f32)
            rest = raw - high
            mid = rest.astype(bf16).astype(f32)
            return high, mid, rest - mid

        h, m, t = three(jnp.concatenate([src[l, 8:12, :], unit], axis=0))
        zero = jnp.zeros_like(h)
        feat[l] = jnp.concatenate([h, m, t, h, m, h, zero, zero], axis=0).T.astype(bf16)
        geo = own[l, 8:12, :]
        turned = jnp.where(rows < 3, geo * -2.0, 1.0)
        low = jnp.where(rows == 0, geo[3:4, :], 0.0)
        h, m, t = three(jnp.concatenate([turned, low], axis=0))
        target[l] = jnp.concatenate([h, h, h, m, m, t, zero, zero], axis=0).astype(bf16)
        return carry

    lax.fori_loop(0, LEAVES, prepare, 0, unroll=4)
    target[LEAVES] = jnp.zeros_like(target[LEAVES])
    acc[...] = jnp.zeros_like(acc)

    def tiles(step, carry):
        for i in range(UNROLL):
            code = lists[which, step * UNROLL + i]
            l = lax.shift_right_logical(code, 5)
            m = code & 31
            square = jnp.maximum(mm(feat[m], target[l]), 1e-30)
            dist = square * lax.rsqrt(square)
            kern = (LOG2E + dist) * jnp.exp2(-dist)
            high, low = split2(kern)
            s = s16[m]
            acc[l] += mm(s, high) + mm(s, low)
        return carry

    lax.fori_loop(0, (counts[which] + UNROLL - 1) // UNROLL, tiles, 0)
    for l in range(LEAVES):
        out[l] = fold(acc[l]) * (AMPLITUDE / LOG2E)


FAR_STEP = 4
HELD = LEAVES + 1
EMPTY = 32 * HELD


def far_kernel(far_rows, coupling, own_side, other_side, out, table, picked, sems):
    step = pl.program_id(0)

    @pl.when(step == 0)
    def _():
        size = own_side.shape[0]
        copies = [
            pltpu.make_async_copy(part, table.at[pl.ds(i * size, size)], sems.at[i])
            for i, part in enumerate((own_side, other_side))
        ]
        for copy in copies:
            copy.start()
        table[EMPTY] = jnp.zeros((4, 128), f32)
        for copy in copies:
            copy.wait()

    for i in range(FAR_STEP):
        l = step * FAR_STEP + i
        for k in range(16):
            picked[pl.ds(128 * i + k * 8, 8), :] = unpack_rows(table[far_rows[k, l]])
        coefs = [
            [picked[pl.ds(128 * i + p + 64 * h, 8, stride=8), :] for h in range(2)]
            for p in range(PROBES)
        ]
        out[l] = contract(
            lambda t, h: coupling[i, 8 * h : 8 * h + 8, 128 * t : 128 * t + 128], coefs, 2
        )


def down_kernel(
    node_rows, nodes0, nodes1, nodes2, nodes3, node_coupling, transfer, basis, order, far,
    near_a, near_b, near_c, out, table, picked, wide, from_node,
):
    for g, nodes in enumerate((nodes0, nodes1, nodes2, nodes3)):
        table[32 * g : 32 * g + 32] = nodes[...]
    table[128] = jnp.zeros((4, 128), f32)
    for k in range(8):
        picked[pl.ds(k * 8, 8), :] = unpack_rows(table[node_rows[k]])
    coefs = [[picked[pl.ds(p, 8, stride=8), :]] for p in range(PROBES)]
    y = contract(lambda t, h: node_coupling[0, :, 128 * t : 128 * t + 128], coefs, 1)
    low = lane_ids((8, 128)) < 64
    for t in range(32):
        wide[:, 128 * t : 128 * t + 128] = jnp.where(low, y[:, t : t + 1], y[:, 64 + t : 65 + t])
    for p in range(PROBES):
        totals = [jnp.zeros((8, 128), f32)] * 4
        for t in range(32):
            factor = wide[p : p + 1, 128 * t : 128 * t + 128]
            for h in range(4):
                totals[h] += transfer[8 * h : 8 * h + 8, 128 * t : 128 * t + 128] * factor
        for h in range(4):
            from_node[pl.ds(p + 64 * h, 8, stride=8), :] = totals[h] + pltpu.roll(totals[h], 64, 1)

    perm = lane_order()

    def leaf(l, carry):
        near = near_a[l] + near_b[l] + near_c[l]
        leaf_out = (
            reorder(far[l], perm) + from_node[pl.ds(pl.multiple_of(l * 8, 8), 8), :]
        )[:, :RANK]
        high, lower = split2(basis[l])
        leaf16 = pieces(leaf_out)
        total = fold(mm(leaf16, high) + mm(leaf16, lower)) + near
        out[l] = fold(mm_nt(pieces(total), one_hot(order[pl.ds(l, 1), :])))
        return carry

    lax.fori_loop(0, LEAVES, leaf, 0, unroll=8)


VM = pl.BlockSpec(memory_space=pltpu.VMEM)
SM = pl.BlockSpec(memory_space=pltpu.SMEM)
ANY = pl.BlockSpec(memory_space=pl.ANY)


def near_call(which, edge, lists, counts, low_src, high_src, own):
    return pl.pallas_call(
        functools.partial(near_kernel, which),
        out_shape=jax.ShapeDtypeStruct((LEAVES, PROBES, POINTS), f32),
        in_specs=[SM, SM, SM, ANY, ANY, VM],
        out_specs=VM,
        scratch_shapes=[
            pltpu.VMEM((LEAVES, POINTS, 64), bf16),
            pltpu.VMEM((LEAVES + 1, 64, POINTS), bf16),
            pltpu.VMEM((LEAVES, 16, POINTS), bf16),
            pltpu.VMEM((LEAVES + 1, 16, POINTS), f32),
            pltpu.VMEM((LEAVES, 12, POINTS), f32),
            pltpu.SemaphoreType.DMA,
        ],
        compiler_params=pltpu.CompilerParams(vmem_limit_bytes=BIG),
        cost_estimate=pl.CostEstimate(
            flops=12 * 10**9, bytes_accessed=30 * 10**6, transcendentals=8 * 10**6
        ),
        name=f"near_{which}",
    )(edge, lists, counts, low_src, high_src, own)


def body(
    probes, coords, order, basis, transfer, far_list, far_count, far_coupling, node_list,
    node_count, node_coupling, near_list, near_count,
):
    grp, leaf = lax.axis_index("grp"), lax.axis_index("leaf")
    groups, blocks = lax.axis_size("grp"), lax.axis_size("leaf")
    device = grp * blocks + leaf
    lowest, highest = leaf == 0, leaf == blocks - 1
    base = jnp.stack([(device - 1) * LEAVES, lowest, highest]).astype(jnp.int32)
    some = lambda *shape: jax.ShapeDtypeStruct(shape, f32)
    ints = lambda *shape: jax.ShapeDtypeStruct(shape, jnp.int32)

    rows = lambda *shape: pl.BlockSpec((UP_STEP,) + shape, lambda i: (i,) + (0,) * len(shape))
    halo, coef, lists, counts = pl.pallas_call(
        up_kernel,
        grid=(LEAVES // UP_STEP,),
        out_shape=(
            some(LEAVES, 12, POINTS), some(HELD, 4, 128), ints(3, TILE_SLOTS), ints(3),
        ),
        in_specs=[SM, SM, SM, rows(8, POINTS), pl.BlockSpec((3, UP_STEP, POINTS), lambda i: (0, i, 0)), rows(POINTS), rows(RANK, POINTS), ANY],
        out_specs=(VM, VM, SM, SM),
        scratch_shapes=[
            pltpu.VMEM((LEAVES * 8, 128), f32),
            pltpu.VMEM((LEAVES, RANK * RANK), f32),
            pltpu.SemaphoreType.DMA,
        ],
        compiler_params=pltpu.CompilerParams(vmem_limit_bytes=BIG),
        name="up",
    )(base, near_list.T, near_count, probes, coords.transpose(1, 0, 2), order, basis, transfer)

    below = lax.ppermute(halo, "leaf", [(i, i + 1) for i in range(blocks - 1)])
    above = lax.ppermute(halo, "leaf", [(i + 1, i) for i in range(blocks - 1)])

    def place(y, x, c):
        return ((y % 4) * 4 + x % 4) * 2 + c

    everyone = [(y, x, c) for y in range(4) for x in range(4) for c in range(2)]

    def shift(part, dy, dx, dc):
        pairs = [(place(y + dy, x + dx, c ^ dc), place(y, x, c)) for y, x, c in everyone]
        return lax.ppermute(part, "leaf", pairs)

    along_x = [coef] + [shift(coef, 0, i, 0) for i in range(1, 4)]
    near_a = near_call(1, jnp.zeros((1,), jnp.int32), lists, counts, halo, halo, halo)
    *along_x, near_a, below, above = lax.optimization_barrier((*along_x, near_a, below, above))
    line = jnp.concatenate(along_x, axis=0)
    line, lists_b = lax.optimization_barrier((line, lists))
    planes = [line] + [shift(line, i, 0, 0) for i in range(1, 4)]
    near_b = near_call(
        0, lowest.astype(jnp.int32).reshape(1), lists_b, counts, below, above, halo
    )
    *planes, near_b = lax.optimization_barrier((*planes, near_b))
    own_side = jnp.concatenate(planes, axis=0)
    own_side, lists_c = lax.optimization_barrier((own_side, lists_b))
    other_side = shift(own_side, 0, 0, 1)
    near_c = near_call(
        2, (1 - highest.astype(jnp.int32)).reshape(1), lists_c, counts, below, above, halo
    )
    other_side, near_c = lax.optimization_barrier((other_side, near_c))
    nodes = jnp.concatenate(
        [part.reshape(16, HELD, 4, 128)[:, LEAVES] for part in (own_side, other_side)], axis=0
    )
    all_nodes = [nodes] + [
        lax.ppermute(nodes, "grp", [((g + i) % groups, g) for g in range(groups)])
        for i in range(1, groups)
    ]

    def slot_of(block):
        y, x, c = block // 8, (block // 2) % 4, block % 2
        my_y, my_x, my_c = leaf // 8, (leaf // 2) % 4, leaf % 2
        return (c ^ my_c) * 16 + ((y - my_y) % 4) * 4 + (x - my_x) % 4

    local = far_list.T - grp * blocks * LEAVES
    far_rows = jnp.where(
        jnp.arange(far_list.shape[1])[:, None] < far_count[None, :],
        slot_of(local // LEAVES) * HELD + local % LEAVES,
        EMPTY,
    ).astype(jnp.int32)
    node_rows = jnp.where(
        jnp.arange(node_list.shape[1]) < node_count[0],
        (node_list[0] // blocks - grp) % groups * blocks + slot_of(node_list[0] % blocks),
        groups * blocks,
    ).astype(jnp.int32)

    far = pl.pallas_call(
        far_kernel,
        grid=(LEAVES // FAR_STEP,),
        out_shape=some(LEAVES, 8, 128),
        in_specs=[SM, pl.BlockSpec((FAR_STEP, 16, RANK * RANK), lambda i: (i, 0, 0))] + [ANY] * 2,
        out_specs=VM,
        scratch_shapes=[
            pltpu.VMEM((EMPTY + 1, 4, 128), f32),
            pltpu.VMEM((FAR_STEP * 128, 128), f32),
            pltpu.SemaphoreType.DMA((2,)),
        ],
        compiler_params=pltpu.CompilerParams(vmem_limit_bytes=BIG),
        cost_estimate=pl.CostEstimate(
            flops=12 * 10**9, bytes_accessed=20 * 10**6, transcendentals=0
        ),
        name="far",
    )(far_rows, far_coupling, own_side, other_side)

    return pl.pallas_call(
        down_kernel,
        out_shape=some(LEAVES, PROBES, POINTS),
        in_specs=[SM] + [VM] * 12,
        out_specs=VM,
        scratch_shapes=[
            pltpu.VMEM((129, 4, 128), f32),
            pltpu.VMEM((64, 128), f32),
            pltpu.VMEM((8, RANK * RANK), f32),
            pltpu.VMEM((LEAVES * 8, 128), f32),
        ],
        compiler_params=pltpu.CompilerParams(vmem_limit_bytes=BIG),
        name="down",
    )(
        node_rows, *all_nodes, node_coupling, transfer, basis, order, far, near_a, near_b, near_c
    )


def solution(mesh):
    rows = ("grp", "leaf")
    return jax.shard_map(
        body,
        mesh=mesh,
        in_specs=(
            P(rows, None, None), P(rows, None, None), P(rows, None), P(rows, None, None),
            P(rows, None), P(rows, None), P(rows), P(rows, None, None), P(rows, None), P(rows),
            P(rows, None, None), P(rows, None), P(rows),
        ),
        out_specs=P(rows, None, None),
        check_vma=False,
    )
```

```python
import functools
import math

import jax
import jax.numpy as jnp
from jax import lax
from jax.experimental import pallas as pl
from jax.experimental.pallas import tpu as pltpu
from jax.sharding import PartitionSpec as P

f32 = jnp.float32
bf16 = jnp.bfloat16
LOG2E = 1.0 / math.log(2.0)
AMPLITUDE = 0.0625
COORD_SCALE = math.sqrt(3.0) / 0.15 * LOG2E
LEAVES = 32
PROBES = 8
POINTS = 256
RANK = 64
UNROLL = 8
TILE_SLOTS = 264
BIG = 20 * 2**20

NT = (((1,), (1,)), ((), ()))


def split2(x):
    high = x.astype(bf16)
    return high, (x - high.astype(f32)).astype(bf16)


def pieces(x):
    high, low = split2(x)
    return jnp.concatenate([high, low], axis=0)


def fold(x):
    half = x.shape[0] // 2
    return x[:half] + x[half:]


def mm(a, b):
    return jnp.dot(a, b, preferred_element_type=f32)


def mm_nt(a, b):
    return lax.dot_general(a, b, NT, preferred_element_type=f32)


def lane_ids(shape):
    return lax.broadcasted_iota(jnp.int32, shape, len(shape) - 1)


def contract(tile, coefs, steps):
    sub = lax.broadcasted_iota(jnp.int32, (8, 128), 0)
    lane = lane_ids((8, 128))

    def over_slots(t):
        blocks = [tile(t, h) for h in range(steps)]
        vs = []
        for p in range(PROBES):
            total = blocks[0] * coefs[p][0]
            for h in range(1, steps):
                total = total + blocks[h] * coefs[p][h]
            vs.append(total)
        for dist in (1, 2, 4):
            keep = (sub & dist) == 0
            vs = [
                jnp.where(keep, a, b) + pltpu.roll(jnp.where(keep, b, a), dist, 0)
                for a, b in zip(vs[0::2], vs[1::2])
            ]
        return vs[0]

    def over_lanes(t0, bits):
        if bits == 0:
            return over_slots(t0)
        dist = 1 << (bits - 1)
        a = over_lanes(t0, bits - 1)
        b = over_lanes(t0 + dist, bits - 1)
        return jnp.where(
            (lane & dist) == 0, a + pltpu.roll(a, 128 - dist, 1), b + pltpu.roll(b, dist, 1)
        )

    y = over_lanes(0, 5)
    return y + pltpu.roll(y, 96, 1)


def lane_order():
    src = lax.broadcasted_iota(jnp.int32, (128, 128), 0)
    dst = lane_ids((128, 128))
    want = (dst & 1) * 64 + ((dst & 63) >> 1)
    return jnp.where(src == want, 1.0, 0.0).astype(bf16)


def reorder(y, perm):
    return fold(mm(pieces(y), perm))


def pack_rows(y):
    return jnp.where(lane_ids((4, 128)) < 64, y[:4], y[4:])


def unpack_rows(v):
    turned = pltpu.roll(v, 64, 1)
    low = lane_ids((4, 128)) < 64
    return jnp.concatenate([jnp.where(low, v, turned), jnp.where(low, turned, v)], axis=0)


def one_hot(order_row):
    rows = lax.broadcasted_iota(jnp.int32, (POINTS, POINTS), 0)
    return jnp.where(rows == order_row, 1.0, 0.0).astype(bf16)


CHUNK = 8
ROUNDS_A = 7
ROUNDS_B = 8


def three(raw):
    high = raw.astype(bf16).astype(f32)
    rest = raw - high
    mid = rest.astype(bf16).astype(f32)
    return high, mid, rest - mid


def unit_rows():
    rows = lax.broadcasted_iota(jnp.int32, (4, POINTS), 0)
    return rows, jnp.where(rows == 0, 1.0, 0.0)


def source_features(geo):
    h, m, t = three(jnp.concatenate([geo, unit_rows()[1]], axis=0))
    zero = jnp.zeros_like(h)
    return jnp.concatenate([h, m, t, h, m, h, zero, zero], axis=0).T.astype(bf16)


def target_features(geo):
    rows, _ = unit_rows()
    turned = jnp.where(rows < 3, geo * -2.0, 1.0)
    low = jnp.where(rows == 0, geo[3:4, :], 0.0)
    h, m, t = three(jnp.concatenate([turned, low], axis=0))
    zero = jnp.zeros_like(h)
    return jnp.concatenate([h, h, h, m, m, t, zero, zero], axis=0).astype(bf16)


def up_kernel(
    base_ref, near_list_in, near_count_in, probes_in, coords_in, order_in, basis_in, transfer_in,
    halo, coef, lists, counts, feat, target, s16_out,
    dup, transfer, probes, coords, order, basis, near_list, near_count, sems, few,
):
    chunks = LEAVES // CHUNK
    small = [
        pltpu.make_async_copy(src, dst, few.at[i])
        for i, (src, dst) in enumerate(
            ((near_list_in, near_list), (near_count_in, near_count), (transfer_in, transfer))
        )
    ]
    loads = []
    for j in range(chunks):
        part = pl.ds(j * CHUNK, CHUNK)
        pairs = (
            (probes_in.at[part], probes.at[part]),
            (coords_in.at[:, part], coords.at[:, part]),
            (order_in.at[part], order.at[part]),
            (basis_in.at[part], basis.at[part]),
        )
        loads.append(
            [pltpu.make_async_copy(src, dst, sems.at[j, i]) for i, (src, dst) in enumerate(pairs)]
        )
    for copy in small[:2] + [copy for chunk in loads for copy in chunk] + small[2:]:
        copy.start()
    target[LEAVES] = jnp.zeros_like(target[LEAVES])
    base = base_ref[0]

    def leaf(l, filled):
        p16 = pieces(probes[l])
        s16 = mm(p16, one_hot(order[pl.ds(l, 1), :]))
        xyz = jnp.concatenate([coords[c, pl.ds(l, 1), :] for c in range(3)], axis=0)
        xyz = (xyz - 0.5) * COORD_SCALE
        geo = jnp.concatenate([xyz, jnp.sum(xyz * xyz, axis=0, keepdims=True)], axis=0)
        halo[l] = jnp.concatenate([fold(s16), geo], axis=0)
        feat[l] = source_features(geo)
        target[l] = target_features(geo)
        s16 = s16.astype(bf16)
        s16_out[l] = s16
        high, low = split2(basis[l])
        c = fold(
            mm_nt(s16, jnp.concatenate([high, high], 0))
            + mm_nt(s16, jnp.concatenate([low, low], 0))
        )
        dup[pl.ds(pl.multiple_of(l * 8, 8), 8), :] = c
        coef[l] = pack_rows(c)
        filled = list(filled)
        used = near_count[l]
        for k in range(8):
            row = near_list[k, l] - base
            side = lax.shift_right_logical(row, 5)
            here = side == 1
            code = l * 64 + (row & 31) + jnp.where(side == 2, 32, 0)
            for which, fits in enumerate((here, jnp.logical_not(here))):
                at = filled[which]
                lists[which, at] = code
                filled[which] = at + jnp.where(fits & (k < used), 1, 0)
        return tuple(filled)

    filled = (jnp.int32(0), jnp.int32(0))
    for copy in small[:2]:
        copy.wait()
    for j in range(chunks):
        for copy in loads[j]:
            copy.wait()
        filled = lax.fori_loop(j * CHUNK, (j + 1) * CHUNK, leaf, filled, unroll=4)
    for which in range(2):
        counts[which] = filled[which]
        for pad in range(UNROLL):
            lists[which, filled[which] + pad] = LEAVES * 64
    small[2].wait()
    coefs = [
        [dup[pl.ds(p + 64 * h, 8, stride=8), :] for h in range(4)] for p in range(PROBES)
    ]
    y = contract(
        lambda t, h: transfer[8 * h : 8 * h + 8, 128 * t : 128 * t + 128], coefs, 4
    )
    coef[LEAVES] = pack_rows(reorder(y, lane_order()))


def near_rounds(which, start, stop, lists, feat, target, s16, acc):
    def tiles(step, carry):
        for i in range(UNROLL):
            code = lists[which, step * UNROLL + i]
            l = lax.shift_right_logical(code, 6)
            m = code & 63
            square = jnp.maximum(mm(feat[m], target[l]), 1e-30)
            dist = square * lax.rsqrt(square)
            kern = (LOG2E + dist) * jnp.exp2(-dist)
            high, low = split2(kern)
            s = s16[m]
            acc[l] += mm(s, high) + mm(s, low)
        return carry

    lax.fori_loop(start, stop, tiles, 0)


def near_plan(counts):
    own = (counts[0] + UNROLL - 1) // UNROLL
    far = (counts[1] + UNROLL - 1) // UNROLL
    cut = jnp.minimum(own, ROUNDS_A)
    turn = jnp.minimum(far, jnp.maximum(ROUNDS_B - (own - cut), 0))
    return own, cut, turn, far


def near_finish(acc, out):
    for l in range(LEAVES):
        out[l] = fold(acc[l]) * (AMPLITUDE / LOG2E)


def near_a_kernel(lists, counts, feat, target, s16, out, acc):
    acc[...] = jnp.zeros_like(acc)
    _, cut, _, _ = near_plan(counts)
    near_rounds(0, 0, cut, lists, feat, target, s16, acc)
    near_finish(acc, out)


def near_b_kernel(
    lists, counts, feat, target, s16, below, above, out, halo_feat, halo_s16, acc
):
    acc[...] = jnp.zeros_like(acc)
    own, cut, turn, _ = near_plan(counts)
    near_rounds(0, cut, own, lists, feat, target, s16, acc)
    for side, src in enumerate((below, above)):

        def prepare(l, carry):
            halo_s16[side * LEAVES + l] = pieces(src[l, :8, :])
            halo_feat[side * LEAVES + l] = source_features(src[l, 8:12, :])
            return carry

        lax.fori_loop(0, LEAVES, prepare, 0, unroll=4)
    near_rounds(1, 0, turn, lists, halo_feat, target, halo_s16, acc)
    near_finish(acc, out)


def near_c_kernel(lists, counts, feat, target, s16, out, acc):
    acc[...] = jnp.zeros_like(acc)
    _, _, turn, far = near_plan(counts)
    near_rounds(1, turn, far, lists, feat, target, s16, acc)
    near_finish(acc, out)


FAR_STEP = 4
HELD = LEAVES + 1
EMPTY = 32 * HELD


def far_kernel(
    place_ref, far_list, far_count, coupling, own_side, other_side,
    out, table, picked, spread, lists, used, sems,
):
    step = pl.program_id(0)
    size = own_side.shape[0]
    copies = [
        pltpu.make_async_copy(src, dst, sems.at[i])
        for i, (src, dst) in enumerate((
            (own_side, table.at[pl.ds(0, size)]),
            (other_side, table.at[pl.ds(size, size)]),
            (far_list, lists),
            (far_count, used),
        ))
    ]

    @pl.when(step == 0)
    def _():
        for copy in copies:
            copy.start()
        table[EMPTY] = jnp.zeros((4, 128), f32)
        for copy in copies:
            copy.wait()

    first, my_y, my_x, my_c = (place_ref[i] for i in range(4))
    sub = lax.broadcasted_iota(jnp.int32, (8, 128), 0)
    lane = lane_ids((8, 128))

    def leaf(i, carry):
        l = step * FAR_STEP + i
        at = pl.multiple_of(i * 128, 128)
        for k in range(16):
            local = lists[k, l] - first
            block = lax.shift_right_logical(local, 5)
            y, x, c = lax.shift_right_logical(block, 3), lax.shift_right_logical(block, 1), block
            slot = ((c ^ my_c) & 1) * 16 + ((y - my_y) & 3) * 4 + ((x - my_x) & 3)
            row = jnp.where(k < used[l], slot * HELD + (local & 31), EMPTY)
            picked[pl.ds(at + k * 8, 8), :] = unpack_rows(table[row])
        totals = [None] * 32
        for k in range(16):
            base = pl.multiple_of((i * 2 + k // 8) * 256, 256) + k % 8
            rows = [coupling[pl.ds(base + 64 * th, 8, stride=8), :] for th in range(4)]
            for p in range(PROBES):
                factor = picked[pl.ds(at + k * 8 + p, 1), :]
                for th in range(4):
                    term = rows[th] * factor
                    j = p * 4 + th
                    totals[j] = term if k == 0 else totals[j] + term
        for bit in range(5):
            dist = 1 << bit
            keep = (lane & dist) == 0
            totals = [
                jnp.where(keep, a + pltpu.roll(a, 128 - dist, 1), b + pltpu.roll(b, dist, 1))
                for a, b in zip(totals[0::2], totals[1::2])
            ]
        y = totals[0] + pltpu.roll(totals[0], 96, 1)
        mine = (lax.shift_right_logical(lane, 2) & 7) == sub
        wide = jnp.concatenate([jnp.where(mine, y[t : t + 1, :], 0.0) for t in range(8)], axis=1)
        spread[pl.ds(pl.multiple_of(l * 16, 16), 16), :] = pieces(wide)
        return carry

    lax.fori_loop(0, FAR_STEP, leaf, 0, unroll=2)

    @pl.when(step == LEAVES // FAR_STEP - 1)
    def _():
        src = lax.broadcasted_iota(jnp.int32, (1024, 128), 0)
        dst = lane_ids((1024, 128)) & 63
        half = lax.shift_right_logical(src, 6) & 1
        row = 2 * (8 * (src & 3) + lax.shift_right_logical(src, 7)) + half
        good = (row == dst) & ((src & 32) == 0)
        y = mm(spread[...], jnp.where(good, 1.0, 0.0).astype(bf16))
        y = y.reshape(LEAVES, 2, 8, 128)
        out[...] = y[:, 0] + y[:, 1]


def down_kernel(
    node_rows, nodes0, nodes1, nodes2, nodes3, node_coupling, transfer, basis, order, far,
    near_a, near_b, near_c, out, table, picked, wide, from_node,
):
    for g, nodes in enumerate((nodes0, nodes1, nodes2, nodes3)):
        table[32 * g : 32 * g + 32] = nodes[...]
    table[128] = jnp.zeros((4, 128), f32)
    for k in range(8):
        picked[pl.ds(k * 8, 8), :] = unpack_rows(table[node_rows[k]])
    coefs = [[picked[pl.ds(p, 8, stride=8), :]] for p in range(PROBES)]
    y = contract(lambda t, h: node_coupling[0, :, 128 * t : 128 * t + 128], coefs, 1)
    low = lane_ids((8, 128)) < 64
    for t in range(32):
        wide[:, 128 * t : 128 * t + 128] = jnp.where(low, y[:, t : t + 1], y[:, 64 + t : 65 + t])
    for p in range(PROBES):
        totals = [jnp.zeros((8, 128), f32)] * 4
        for t in range(32):
            factor = wide[p : p + 1, 128 * t : 128 * t + 128]
            for h in range(4):
                totals[h] += transfer[8 * h : 8 * h + 8, 128 * t : 128 * t + 128] * factor
        for h in range(4):
            from_node[pl.ds(p + 64 * h, 8, stride=8), :] = totals[h] + pltpu.roll(totals[h], 64, 1)

    def leaf(l, carry):
        near = near_a[l] + near_b[l] + near_c[l]
        leaf_out = (
            far[l] + from_node[pl.ds(pl.multiple_of(l * 8, 8), 8), :]
        )[:, :RANK]
        high, lower = split2(basis[l])
        leaf16 = pieces(leaf_out)
        total = fold(mm(leaf16, high) + mm(leaf16, lower)) + near
        out[l] = fold(mm_nt(pieces(total), one_hot(order[pl.ds(l, 1), :])))
        return carry

    lax.fori_loop(0, LEAVES, leaf, 0, unroll=8)


VM = pl.BlockSpec(memory_space=pltpu.VMEM)
SM = pl.BlockSpec(memory_space=pltpu.SMEM)
ANY = pl.BlockSpec(memory_space=pl.ANY)


HBM = pl.BlockSpec(memory_space=pltpu.HBM)


def near_call(kernel, extra, name, *args):
    return pl.pallas_call(
        kernel,
        out_shape=(jax.ShapeDtypeStruct((LEAVES, PROBES, POINTS), f32), *extra),
        in_specs=[SM, SM] + [VM] * (len(args) - 2),
        out_specs=(VM,) * (1 + len(extra)),
        scratch_shapes=[pltpu.VMEM((LEAVES + 1, 16, POINTS), f32)],
        compiler_params=pltpu.CompilerParams(vmem_limit_bytes=BIG),
        cost_estimate=pl.CostEstimate(
            flops=12 * 10**9, bytes_accessed=30 * 10**6, transcendentals=8 * 10**6
        ),
        name=name,
    )(*args)


def body(
    probes, coords, order, basis, transfer, far_list, far_count, far_coupling, node_list,
    node_count, node_coupling, near_list, near_count,
):
    grp, leaf = lax.axis_index("grp"), lax.axis_index("leaf")
    groups, blocks = lax.axis_size("grp"), lax.axis_size("leaf")
    device = grp * blocks + leaf
    base = ((device - 1) * LEAVES).reshape(1).astype(jnp.int32)
    some = lambda *shape: jax.ShapeDtypeStruct(shape, f32)
    ints = lambda *shape: jax.ShapeDtypeStruct(shape, jnp.int32)
    short = lambda *shape: jax.ShapeDtypeStruct(shape, bf16)

    halo, coef, lists, counts, feat, target, s16 = pl.pallas_call(
        up_kernel,
        out_shape=(
            some(LEAVES, 12, POINTS), some(HELD, 4, 128), ints(2, TILE_SLOTS), ints(2),
            short(LEAVES, POINTS, 64), short(LEAVES + 1, 64, POINTS), short(LEAVES, 16, POINTS),
        ),
        in_specs=[SM] + [HBM] * 7,
        out_specs=(VM, VM, SM, SM, VM, VM, VM),
        scratch_shapes=[
            pltpu.VMEM((LEAVES * 8, 128), f32),
            pltpu.VMEM((LEAVES, RANK * RANK), f32),
            pltpu.VMEM((LEAVES, PROBES, POINTS), f32),
            pltpu.VMEM((3, LEAVES, POINTS), f32),
            pltpu.VMEM((LEAVES, POINTS), jnp.int32),
            pltpu.VMEM((LEAVES, RANK, POINTS), f32),
            pltpu.SMEM((8, LEAVES), jnp.int32),
            pltpu.SMEM((LEAVES,), jnp.int32),
            pltpu.SemaphoreType.DMA((LEAVES // CHUNK, 4)),
            pltpu.SemaphoreType.DMA((3,)),
        ],
        compiler_params=pltpu.CompilerParams(vmem_limit_bytes=BIG),
        name="up",
    )(
        base,
        *(
            pltpu.with_memory_space_constraint(array, pltpu.HBM)
            for array in (
                near_list.T, near_count, probes, coords.transpose(1, 0, 2), order, basis, transfer
            )
        ),
    )

    below = lax.ppermute(halo, "leaf", [(i, i + 1) for i in range(blocks - 1)])
    above = lax.ppermute(halo, "leaf", [(i + 1, i) for i in range(blocks - 1)])

    def place(y, x, c):
        return ((y % 4) * 4 + x % 4) * 2 + c

    everyone = [(y, x, c) for y in range(4) for x in range(4) for c in range(2)]

    def shift(part, dy, dx, dc):
        pairs = [(place(y + dy, x + dx, c ^ dc), place(y, x, c)) for y, x, c in everyone]
        return lax.ppermute(part, "leaf", pairs)

    along_x = [coef] + [shift(coef, 0, i, 0) for i in range(1, 4)]
    near_a = near_call(near_a_kernel, (), "near_a", lists, counts, feat, target, s16)[0]
    *along_x, near_a, below, above = lax.optimization_barrier((*along_x, near_a, below, above))
    line = jnp.concatenate(along_x, axis=0)
    line, lists_b = lax.optimization_barrier((line, lists))
    planes = [line] + [shift(line, i, 0, 0) for i in range(1, 4)]
    near_b, halo_feat, halo_s16 = near_call(
        near_b_kernel,
        (short(2 * LEAVES, POINTS, 64), short(2 * LEAVES, 16, POINTS)),
        "near_b", lists_b, counts, feat, target, s16, below, above,
    )
    *planes, near_b = lax.optimization_barrier((*planes, near_b))
    own_side = jnp.concatenate(planes, axis=0)
    own_side, lists_c = lax.optimization_barrier((own_side, lists_b))
    other_side = shift(own_side, 0, 0, 1)
    near_c = near_call(
        near_c_kernel, (), "near_c", lists_c, counts, halo_feat, target, halo_s16
    )[0]
    other_side, near_c = lax.optimization_barrier((other_side, near_c))
    nodes = jnp.concatenate(
        [part.reshape(16, HELD, 4, 128)[:, LEAVES] for part in (own_side, other_side)], axis=0
    )
    all_nodes = [nodes] + [
        lax.ppermute(nodes, "grp", [((g + i) % groups, g) for g in range(groups)])
        for i in range(1, groups)
    ]

    def slot_of(block):
        y, x, c = block // 8, (block // 2) % 4, block % 2
        my_y, my_x, my_c = leaf // 8, (leaf // 2) % 4, leaf % 2
        return (c ^ my_c) * 16 + ((y - my_y) % 4) * 4 + (x - my_x) % 4

    node_rows = jnp.where(
        jnp.arange(node_list.shape[1]) < node_count[0],
        (node_list[0] // blocks - grp) % groups * blocks + slot_of(node_list[0] % blocks),
        groups * blocks,
    ).astype(jnp.int32)

    lying = far_coupling.reshape(LEAVES, 2, 8, 32, 128).transpose(0, 1, 3, 2, 4).reshape(-1, 128)
    spot = jnp.stack([grp * blocks * LEAVES, leaf // 8, (leaf // 2) % 4, leaf % 2]).astype(jnp.int32)
    far = pl.pallas_call(
        far_kernel,
        grid=(LEAVES // FAR_STEP,),
        out_shape=some(LEAVES, 8, 128),
        in_specs=[SM, ANY, ANY, pl.BlockSpec((FAR_STEP * 512, 128), lambda i: (i, 0)), ANY, ANY],
        out_specs=VM,
        scratch_shapes=[
            pltpu.VMEM((EMPTY + 1, 4, 128), f32),
            pltpu.VMEM((FAR_STEP * 128, 128), f32),
            pltpu.VMEM((LEAVES * 16, 1024), bf16),
            pltpu.SMEM((16, LEAVES), jnp.int32),
            pltpu.SMEM((LEAVES,), jnp.int32),
            pltpu.SemaphoreType.DMA((4,)),
        ],
        compiler_params=pltpu.CompilerParams(vmem_limit_bytes=BIG),
        cost_estimate=pl.CostEstimate(
            flops=12 * 10**9, bytes_accessed=20 * 10**6, transcendentals=0
        ),
        name="far",
    )(
        spot,
        pltpu.with_memory_space_constraint(far_list.T, pltpu.HBM),
        pltpu.with_memory_space_constraint(far_count, pltpu.HBM),
        lying, own_side, other_side,
    )

    return pl.pallas_call(
        down_kernel,
        out_shape=some(LEAVES, PROBES, POINTS),
        in_specs=[SM] + [VM] * 12,
        out_specs=VM,
        scratch_shapes=[
            pltpu.VMEM((129, 4, 128), f32),
            pltpu.VMEM((64, 128), f32),
            pltpu.VMEM((8, RANK * RANK), f32),
            pltpu.VMEM((LEAVES * 8, 128), f32),
        ],
        compiler_params=pltpu.CompilerParams(vmem_limit_bytes=BIG),
        name="down",
    )(
        node_rows, *all_nodes, node_coupling, transfer, basis, order, far, near_a, near_b, near_c
    )


def solution(mesh):
    rows = ("grp", "leaf")
    return jax.shard_map(
        body,
        mesh=mesh,
        in_specs=(
            P(rows, None, None), P(rows, None, None), P(rows, None), P(rows, None, None),
            P(rows, None), P(rows, None), P(rows), P(rows, None, None), P(rows, None), P(rows),
            P(rows, None, None), P(rows, None), P(rows),
        ),
        out_specs=P(rows, None, None),
        check_vma=False,
    )
```

```python
import functools
import math

import jax
import jax.numpy as jnp
from jax import lax
from jax.experimental import pallas as pl
from jax.experimental.pallas import tpu as pltpu
from jax.sharding import PartitionSpec as P

f32 = jnp.float32
bf16 = jnp.bfloat16
LOG2E = 1.0 / math.log(2.0)
AMPLITUDE = 0.0625
COORD_SCALE = math.sqrt(3.0) / 0.15 * LOG2E
LEAVES = 32
PROBES = 8
POINTS = 256
RANK = 64
UNROLL = 8
TILE_SLOTS = 264
BIG = 20 * 2**20

NT = (((1,), (1,)), ((), ()))


def split2(x):
    high = x.astype(bf16)
    return high, (x - high.astype(f32)).astype(bf16)


def pieces(x):
    high, low = split2(x)
    return jnp.concatenate([high, low], axis=0)


def fold(x):
    half = x.shape[0] // 2
    return x[:half] + x[half:]


def mm(a, b):
    return jnp.dot(a, b, preferred_element_type=f32)


def mm_nt(a, b):
    return lax.dot_general(a, b, NT, preferred_element_type=f32)


def lane_ids(shape):
    return lax.broadcasted_iota(jnp.int32, shape, len(shape) - 1)


def contract(tile, coefs, steps):
    sub = lax.broadcasted_iota(jnp.int32, (8, 128), 0)
    lane = lane_ids((8, 128))

    def over_slots(t):
        blocks = [tile(t, h) for h in range(steps)]
        vs = []
        for p in range(PROBES):
            total = blocks[0] * coefs[p][0]
            for h in range(1, steps):
                total = total + blocks[h] * coefs[p][h]
            vs.append(total)
        for dist in (1, 2, 4):
            keep = (sub & dist) == 0
            vs = [
                jnp.where(keep, a, b) + pltpu.roll(jnp.where(keep, b, a), dist, 0)
                for a, b in zip(vs[0::2], vs[1::2])
            ]
        return vs[0]

    def over_lanes(t0, bits):
        if bits == 0:
            return over_slots(t0)
        dist = 1 << (bits - 1)
        a = over_lanes(t0, bits - 1)
        b = over_lanes(t0 + dist, bits - 1)
        return jnp.where(
            (lane & dist) == 0, a + pltpu.roll(a, 128 - dist, 1), b + pltpu.roll(b, dist, 1)
        )

    y = over_lanes(0, 5)
    return y + pltpu.roll(y, 96, 1)


def lane_order():
    src = lax.broadcasted_iota(jnp.int32, (128, 128), 0)
    dst = lane_ids((128, 128))
    want = (dst & 1) * 64 + ((dst & 63) >> 1)
    return jnp.where(src == want, 1.0, 0.0).astype(bf16)


def reorder(y, perm):
    return fold(mm(pieces(y), perm))


def pack_rows(y):
    return jnp.where(lane_ids((4, 128)) < 64, y[:4], y[4:])


def unpack_rows(v):
    turned = pltpu.roll(v, 64, 1)
    low = lane_ids((4, 128)) < 64
    return jnp.concatenate([jnp.where(low, v, turned), jnp.where(low, turned, v)], axis=0)


def one_hot(order_row):
    rows = lax.broadcasted_iota(jnp.int32, (POINTS, POINTS), 0)
    return jnp.where(rows == order_row, 1.0, 0.0).astype(bf16)


CHUNK = 8
ROUNDS_A = 7
ROUNDS_B = 8


def three(raw):
    high = raw.astype(bf16).astype(f32)
    rest = raw - high
    mid = rest.astype(bf16).astype(f32)
    return high, mid, rest - mid


def unit_rows():
    rows = lax.broadcasted_iota(jnp.int32, (4, POINTS), 0)
    return rows, jnp.where(rows == 0, 1.0, 0.0)


def source_features(geo):
    h, m, t = three(jnp.concatenate([geo, unit_rows()[1]], axis=0))
    zero = jnp.zeros_like(h)
    return jnp.concatenate([h, m, t, h, m, h, zero, zero], axis=0).T.astype(bf16)


def target_features(geo):
    rows, _ = unit_rows()
    turned = jnp.where(rows < 3, geo * -2.0, 1.0)
    low = jnp.where(rows == 0, geo[3:4, :], 0.0)
    h, m, t = three(jnp.concatenate([turned, low], axis=0))
    zero = jnp.zeros_like(h)
    return jnp.concatenate([h, h, h, m, m, t, zero, zero], axis=0).astype(bf16)


def up_kernel(
    base_ref, near_list_in, near_count_in, probes_in, coords_in, order_in, basis_in, transfer_in,
    halo, coef, lists, counts, feat, target, s16_out,
    dup, transfer, probes, coords, order, basis, near_list, near_count, sems, few,
):
    chunks = LEAVES // CHUNK
    small = [
        pltpu.make_async_copy(src, dst, few.at[i])
        for i, (src, dst) in enumerate(
            ((near_list_in, near_list), (near_count_in, near_count), (transfer_in, transfer))
        )
    ]
    loads = []
    for j in range(chunks):
        part = pl.ds(j * CHUNK, CHUNK)
        pairs = (
            (probes_in.at[part], probes.at[part]),
            (coords_in.at[:, part], coords.at[:, part]),
            (order_in.at[part], order.at[part]),
            (basis_in.at[part], basis.at[part]),
        )
        loads.append(
            [pltpu.make_async_copy(src, dst, sems.at[j, i]) for i, (src, dst) in enumerate(pairs)]
        )
    for copy in small[:2] + [copy for chunk in loads for copy in chunk] + small[2:]:
        copy.start()
    target[LEAVES] = jnp.zeros_like(target[LEAVES])
    base = base_ref[0]

    def leaf(l, filled):
        p16 = pieces(probes[l])
        s16 = mm(p16, one_hot(order[pl.ds(l, 1), :]))
        xyz = jnp.concatenate([coords[c, pl.ds(l, 1), :] for c in range(3)], axis=0)
        xyz = (xyz - 0.5) * COORD_SCALE
        geo = jnp.concatenate([xyz, jnp.sum(xyz * xyz, axis=0, keepdims=True)], axis=0)
        halo[l] = jnp.concatenate([fold(s16), geo], axis=0)
        feat[l] = source_features(geo)
        target[l] = target_features(geo)
        s16 = s16.astype(bf16)
        s16_out[l] = s16
        high, low = split2(basis[l])
        c = fold(
            mm_nt(s16, jnp.concatenate([high, high], 0))
            + mm_nt(s16, jnp.concatenate([low, low], 0))
        )
        dup[pl.ds(pl.multiple_of(l * 8, 8), 8), :] = c
        coef[l] = pack_rows(c)
        filled = list(filled)
        used = near_count[l]
        for k in range(8):
            row = near_list[k, l] - base
            side = lax.shift_right_logical(row, 5)
            here = side == 1
            code = l * 64 + (row & 31) + jnp.where(side == 2, 32, 0)
            for which, fits in enumerate((here, jnp.logical_not(here))):
                at = filled[which]
                lists[which, at] = code
                filled[which] = at + jnp.where(fits & (k < used), 1, 0)
        return tuple(filled)

    filled = (jnp.int32(0), jnp.int32(0))
    for copy in small[:2]:
        copy.wait()
    for j in range(chunks):
        for copy in loads[j]:
            copy.wait()
        filled = lax.fori_loop(j * CHUNK, (j + 1) * CHUNK, leaf, filled, unroll=4)
    for which in range(2):
        counts[which] = filled[which]
        for pad in range(UNROLL):
            lists[which, filled[which] + pad] = LEAVES * 64
    small[2].wait()
    coefs = [
        [dup[pl.ds(p + 64 * h, 8, stride=8), :] for h in range(4)] for p in range(PROBES)
    ]
    y = contract(
        lambda t, h: transfer[8 * h : 8 * h + 8, 128 * t : 128 * t + 128], coefs, 4
    )
    coef[LEAVES] = pack_rows(reorder(y, lane_order()))


def near_rounds(which, start, stop, lists, feat, target, s16, acc):
    def tiles(step, carry):
        for i in range(UNROLL):
            code = lists[which, step * UNROLL + i]
            l = lax.shift_right_logical(code, 6)
            m = code & 63
            square = jnp.maximum(mm(feat[m], target[l]), 1e-30)
            dist = square * lax.rsqrt(square)
            kern = (LOG2E + dist) * jnp.exp2(-dist)
            high, low = split2(kern)
            s = s16[m]
            acc[l] += mm(s, high) + mm(s, low)
        return carry

    lax.fori_loop(start, stop, tiles, 0)


def near_plan(counts):
    own = (counts[0] + UNROLL - 1) // UNROLL
    far = (counts[1] + UNROLL - 1) // UNROLL
    cut = jnp.minimum(own, ROUNDS_A)
    turn = jnp.minimum(far, jnp.maximum(ROUNDS_B - (own - cut), 0))
    return own, cut, turn, far


def near_finish(acc, out):
    for l in range(LEAVES):
        out[l] = fold(acc[l]) * (AMPLITUDE / LOG2E)


def near_a_kernel(lists, counts, feat, target, s16, out, acc):
    acc[...] = jnp.zeros_like(acc)
    _, cut, _, _ = near_plan(counts)
    near_rounds(0, 0, cut, lists, feat, target, s16, acc)
    near_finish(acc, out)


def near_b_kernel(
    lists, counts, feat, target, s16, below, above, out, halo_feat, halo_s16, acc
):
    acc[...] = jnp.zeros_like(acc)
    own, cut, turn, _ = near_plan(counts)
    near_rounds(0, cut, own, lists, feat, target, s16, acc)
    for side, src in enumerate((below, above)):

        def prepare(l, carry):
            halo_s16[side * LEAVES + l] = pieces(src[l, :8, :])
            halo_feat[side * LEAVES + l] = source_features(src[l, 8:12, :])
            return carry

        lax.fori_loop(0, LEAVES, prepare, 0, unroll=4)
    near_rounds(1, 0, turn, lists, halo_feat, target, halo_s16, acc)
    near_finish(acc, out)


def near_c_kernel(lists, counts, feat, target, s16, out, acc):
    acc[...] = jnp.zeros_like(acc)
    _, _, turn, far = near_plan(counts)
    near_rounds(1, turn, far, lists, feat, target, s16, acc)
    near_finish(acc, out)


FAR_STEP = 8
FAR_UNROLL = 8
HELD = LEAVES + 1
EMPTY = 32 * HELD


def far_kernel(
    place_ref, far_list, far_count, coupling, own_side, other_side,
    out, table, picked, y_all, lists, used, sems,
):
    step = pl.program_id(0)
    size = own_side.shape[0]
    copies = [
        pltpu.make_async_copy(src, dst, sems.at[i])
        for i, (src, dst) in enumerate((
            (own_side, table.at[pl.ds(0, size)]),
            (other_side, table.at[pl.ds(size, size)]),
            (far_list, lists),
            (far_count, used),
        ))
    ]

    @pl.when(step == 0)
    def _():
        for copy in copies:
            copy.start()
        table[EMPTY] = jnp.zeros((4, 128), f32)
        for copy in copies:
            copy.wait()

    first, my_y, my_x, my_c = (place_ref[i] for i in range(4))
    low = lane_ids((4, 128)) < 64

    def leaf(i, carry):
        l = step * FAR_STEP + i
        at = pl.multiple_of(i * 256, 256)
        for k in range(16):
            local = lists[k, l] - first
            block = lax.shift_right_logical(local, 5)
            y, x, c = lax.shift_right_logical(block, 3), lax.shift_right_logical(block, 1), block
            slot = ((c ^ my_c) & 1) * 16 + ((y - my_y) & 3) * 4 + ((x - my_x) & 3)
            row = jnp.where(k < used[l], slot * HELD + (local & 31), EMPTY)
            held = table[row]
            turned = pltpu.roll(held, 64, 1)
            for j, (left, right) in enumerate(((held, 0.0), (turned, 0.0), (0.0, turned), (0.0, held))):
                picked[pl.ds(at + k * 16 + 4 * j, 4), :] = jnp.where(low, left, right)
        coefs = jnp.concatenate([picked[pl.ds(at + k * 16, 16), :] for k in range(16)], axis=1)
        blocks = []
        for k in range(16):
            base = pl.multiple_of((i * 2 + k // 8) * 256, 256) + k % 8
            blocks.append(coupling[pl.ds(base, 32, stride=8), :])
        high, lower = split2(jnp.concatenate(blocks, axis=1))
        c16 = pieces(coefs)
        y = fold(mm_nt(c16, high) + mm_nt(c16, lower))
        gap = jnp.zeros((8, 32), f32)
        y_all[pl.ds(pl.multiple_of(l * 16, 16), 16), :] = pieces(
            jnp.concatenate([y[:8], gap, y[8:], gap], axis=1)
        )
        return carry

    lax.fori_loop(0, FAR_STEP, leaf, 0, unroll=FAR_UNROLL)

    @pl.when(step == LEAVES // FAR_STEP - 1)
    def _():
        y = mm(y_all[...], lane_order()).reshape(LEAVES, 2, 8, 128)
        out[...] = y[:, 0] + y[:, 1]


def down_kernel(
    node_rows, nodes0, nodes1, nodes2, nodes3, node_coupling, transfer, basis, order, far,
    near_a, near_b, near_c, out, table, picked, wide, from_node,
):
    for g, nodes in enumerate((nodes0, nodes1, nodes2, nodes3)):
        table[32 * g : 32 * g + 32] = nodes[...]
    table[128] = jnp.zeros((4, 128), f32)
    for k in range(8):
        picked[pl.ds(k * 8, 8), :] = unpack_rows(table[node_rows[k]])
    coefs = [[picked[pl.ds(p, 8, stride=8), :]] for p in range(PROBES)]
    y = contract(lambda t, h: node_coupling[0, :, 128 * t : 128 * t + 128], coefs, 1)
    low = lane_ids((8, 128)) < 64
    for t in range(32):
        wide[:, 128 * t : 128 * t + 128] = jnp.where(low, y[:, t : t + 1], y[:, 64 + t : 65 + t])
    for p in range(PROBES):
        totals = [jnp.zeros((8, 128), f32)] * 4
        for t in range(32):
            factor = wide[p : p + 1, 128 * t : 128 * t + 128]
            for h in range(4):
                totals[h] += transfer[8 * h : 8 * h + 8, 128 * t : 128 * t + 128] * factor
        for h in range(4):
            from_node[pl.ds(p + 64 * h, 8, stride=8), :] = totals[h] + pltpu.roll(totals[h], 64, 1)

    def leaf(l, carry):
        near = near_a[l] + near_b[l] + near_c[l]
        leaf_out = (
            far[l] + from_node[pl.ds(pl.multiple_of(l * 8, 8), 8), :]
        )[:, :RANK]
        high, lower = split2(basis[l])
        leaf16 = pieces(leaf_out)
        total = fold(mm(leaf16, high) + mm(leaf16, lower)) + near
        out[l] = fold(mm_nt(pieces(total), one_hot(order[pl.ds(l, 1), :])))
        return carry

    lax.fori_loop(0, LEAVES, leaf, 0, unroll=8)


VM = pl.BlockSpec(memory_space=pltpu.VMEM)
SM = pl.BlockSpec(memory_space=pltpu.SMEM)
ANY = pl.BlockSpec(memory_space=pl.ANY)


HBM = pl.BlockSpec(memory_space=pltpu.HBM)


def near_call(kernel, extra, name, *args):
    return pl.pallas_call(
        kernel,
        out_shape=(jax.ShapeDtypeStruct((LEAVES, PROBES, POINTS), f32), *extra),
        in_specs=[SM, SM] + [VM] * (len(args) - 2),
        out_specs=(VM,) * (1 + len(extra)),
        scratch_shapes=[pltpu.VMEM((LEAVES + 1, 16, POINTS), f32)],
        compiler_params=pltpu.CompilerParams(vmem_limit_bytes=BIG),
        cost_estimate=pl.CostEstimate(
            flops=12 * 10**9, bytes_accessed=30 * 10**6, transcendentals=8 * 10**6
        ),
        name=name,
    )(*args)


def body(
    probes, coords, order, basis, transfer, far_list, far_count, far_coupling, node_list,
    node_count, node_coupling, near_list, near_count,
):
    grp, leaf = lax.axis_index("grp"), lax.axis_index("leaf")
    groups, blocks = lax.axis_size("grp"), lax.axis_size("leaf")
    device = grp * blocks + leaf
    base = ((device - 1) * LEAVES).reshape(1).astype(jnp.int32)
    some = lambda *shape: jax.ShapeDtypeStruct(shape, f32)
    ints = lambda *shape: jax.ShapeDtypeStruct(shape, jnp.int32)
    short = lambda *shape: jax.ShapeDtypeStruct(shape, bf16)

    halo, coef, lists, counts, feat, target, s16 = pl.pallas_call(
        up_kernel,
        out_shape=(
            some(LEAVES, 12, POINTS), some(HELD, 4, 128), ints(2, TILE_SLOTS), ints(2),
            short(LEAVES, POINTS, 64), short(LEAVES + 1, 64, POINTS), short(LEAVES, 16, POINTS),
        ),
        in_specs=[SM] + [HBM] * 7,
        out_specs=(VM, VM, SM, SM, VM, VM, VM),
        scratch_shapes=[
            pltpu.VMEM((LEAVES * 8, 128), f32),
            pltpu.VMEM((LEAVES, RANK * RANK), f32),
            pltpu.VMEM((LEAVES, PROBES, POINTS), f32),
            pltpu.VMEM((3, LEAVES, POINTS), f32),
            pltpu.VMEM((LEAVES, POINTS), jnp.int32),
            pltpu.VMEM((LEAVES, RANK, POINTS), f32),
            pltpu.SMEM((8, LEAVES), jnp.int32),
            pltpu.SMEM((LEAVES,), jnp.int32),
            pltpu.SemaphoreType.DMA((LEAVES // CHUNK, 4)),
            pltpu.SemaphoreType.DMA((3,)),
        ],
        compiler_params=pltpu.CompilerParams(vmem_limit_bytes=BIG),
        name="up",
    )(
        base,
        *(
            pltpu.with_memory_space_constraint(array, pltpu.HBM)
            for array in (
                near_list.T, near_count, probes, coords.transpose(1, 0, 2), order, basis, transfer
            )
        ),
    )

    below = lax.ppermute(halo, "leaf", [(i, (i + 1) % blocks) for i in range(blocks)])
    above = lax.ppermute(halo, "leaf", [((i + 1) % blocks, i) for i in range(blocks)])

    def place(y, x, c):
        return ((y % 4) * 4 + x % 4) * 2 + c

    everyone = [(y, x, c) for y in range(4) for x in range(4) for c in range(2)]

    def shift(part, dy, dx, dc):
        pairs = [(place(y + dy, x + dx, c ^ dc), place(y, x, c)) for y, x, c in everyone]
        return lax.ppermute(part, "leaf", pairs)

    along_x = [coef] + [shift(coef, 0, i, 0) for i in range(1, 4)]
    near_a = near_call(near_a_kernel, (), "near_a", lists, counts, feat, target, s16)[0]
    *along_x, near_a, below, above = lax.optimization_barrier((*along_x, near_a, below, above))
    line = jnp.concatenate(along_x, axis=0)
    line, lists_b = lax.optimization_barrier((line, lists))
    planes = [line] + [shift(line, i, 0, 0) for i in range(1, 4)]
    near_b, halo_feat, halo_s16 = near_call(
        near_b_kernel,
        (short(2 * LEAVES, POINTS, 64), short(2 * LEAVES, 16, POINTS)),
        "near_b", lists_b, counts, feat, target, s16, below, above,
    )
    *planes, near_b = lax.optimization_barrier((*planes, near_b))
    own_side = jnp.concatenate(planes, axis=0)
    own_side, lists_c = lax.optimization_barrier((own_side, lists_b))
    other_side = shift(own_side, 0, 0, 1)
    near_c = near_call(
        near_c_kernel, (), "near_c", lists_c, counts, halo_feat, target, halo_s16
    )[0]
    other_side, near_c = lax.optimization_barrier((other_side, near_c))
    nodes = jnp.concatenate(
        [part.reshape(16, HELD, 4, 128)[:, LEAVES] for part in (own_side, other_side)], axis=0
    )
    all_nodes = [nodes] + [
        lax.ppermute(nodes, "grp", [((g + i) % groups, g) for g in range(groups)])
        for i in range(1, groups)
    ]

    def slot_of(block):
        y, x, c = block // 8, (block // 2) % 4, block % 2
        my_y, my_x, my_c = leaf // 8, (leaf // 2) % 4, leaf % 2
        return (c ^ my_c) * 16 + ((y - my_y) % 4) * 4 + (x - my_x) % 4

    node_rows = jnp.where(
        jnp.arange(node_list.shape[1]) < node_count[0],
        (node_list[0] // blocks - grp) % groups * blocks + slot_of(node_list[0] % blocks),
        groups * blocks,
    ).astype(jnp.int32)

    lying = far_coupling.reshape(LEAVES, 2, 8, 32, 128).transpose(0, 1, 3, 2, 4).reshape(-1, 128)
    spot = jnp.stack([grp * blocks * LEAVES, leaf // 8, (leaf // 2) % 4, leaf % 2]).astype(jnp.int32)
    far = pl.pallas_call(
        far_kernel,
        grid=(LEAVES // FAR_STEP,),
        out_shape=some(LEAVES, 8, 128),
        in_specs=[SM, ANY, ANY, pl.BlockSpec((FAR_STEP * 512, 128), lambda i: (i, 0)), ANY, ANY],
        out_specs=VM,
        scratch_shapes=[
            pltpu.VMEM((EMPTY + 1, 4, 128), f32),
            pltpu.VMEM((FAR_STEP * 256, 128), f32),
            pltpu.VMEM((LEAVES * 16, 128), bf16),
            pltpu.SMEM((16, LEAVES), jnp.int32),
            pltpu.SMEM((LEAVES,), jnp.int32),
            pltpu.SemaphoreType.DMA((4,)),
        ],
        compiler_params=pltpu.CompilerParams(vmem_limit_bytes=BIG),
        cost_estimate=pl.CostEstimate(
            flops=12 * 10**9, bytes_accessed=20 * 10**6, transcendentals=0
        ),
        name="far",
    )(
        spot,
        pltpu.with_memory_space_constraint(far_list.T, pltpu.HBM),
        pltpu.with_memory_space_constraint(far_count, pltpu.HBM),
        lying, own_side, other_side,
    )

    return pl.pallas_call(
        down_kernel,
        out_shape=some(LEAVES, PROBES, POINTS),
        in_specs=[SM] + [VM] * 12,
        out_specs=VM,
        scratch_shapes=[
            pltpu.VMEM((129, 4, 128), f32),
            pltpu.VMEM((64, 128), f32),
            pltpu.VMEM((8, RANK * RANK), f32),
            pltpu.VMEM((LEAVES * 8, 128), f32),
        ],
        compiler_params=pltpu.CompilerParams(vmem_limit_bytes=BIG),
        name="down",
    )(
        node_rows, *all_nodes, node_coupling, transfer, basis, order, far, near_a, near_b, near_c
    )


def solution(mesh):
    rows = ("grp", "leaf")
    return jax.shard_map(
        body,
        mesh=mesh,
        in_specs=(
            P(rows, None, None), P(rows, None, None), P(rows, None), P(rows, None, None),
            P(rows, None), P(rows, None), P(rows), P(rows, None, None), P(rows, None), P(rows),
            P(rows, None, None), P(rows, None), P(rows),
        ),
        out_specs=P(rows, None, None),
        check_vma=False,
    )
```

```python
import functools
import math

import jax
import jax.numpy as jnp
from jax import lax
from jax.experimental import pallas as pl
from jax.experimental.pallas import tpu as pltpu
from jax.sharding import PartitionSpec as P

f32 = jnp.float32
bf16 = jnp.bfloat16
LOG2E = 1.0 / math.log(2.0)
AMPLITUDE = 0.0625
COORD_SCALE = math.sqrt(3.0) / 0.15 * LOG2E
LEAVES = 32
PROBES = 8
POINTS = 256
RANK = 64
UNROLL = 8
TILE_SLOTS = 264
BIG = 20 * 2**20

NT = (((1,), (1,)), ((), ()))


def split2(x):
    high = x.astype(bf16)
    return high, (x - high.astype(f32)).astype(bf16)


def pieces(x):
    high, low = split2(x)
    return jnp.concatenate([high, low], axis=0)


def fold(x):
    half = x.shape[0] // 2
    return x[:half] + x[half:]


def mm(a, b):
    return jnp.dot(a, b, preferred_element_type=f32)


def mm_nt(a, b):
    return lax.dot_general(a, b, NT, preferred_element_type=f32)


def lane_ids(shape):
    return lax.broadcasted_iota(jnp.int32, shape, len(shape) - 1)


def contract(tile, coefs, steps):
    sub = lax.broadcasted_iota(jnp.int32, (8, 128), 0)
    lane = lane_ids((8, 128))

    def over_slots(t):
        blocks = [tile(t, h) for h in range(steps)]
        vs = []
        for p in range(PROBES):
            total = blocks[0] * coefs[p][0]
            for h in range(1, steps):
                total = total + blocks[h] * coefs[p][h]
            vs.append(total)
        for dist in (1, 2, 4):
            keep = (sub & dist) == 0
            vs = [
                jnp.where(keep, a, b) + pltpu.roll(jnp.where(keep, b, a), dist, 0)
                for a, b in zip(vs[0::2], vs[1::2])
            ]
        return vs[0]

    def over_lanes(t0, bits):
        if bits == 0:
            return over_slots(t0)
        dist = 1 << (bits - 1)
        a = over_lanes(t0, bits - 1)
        b = over_lanes(t0 + dist, bits - 1)
        return jnp.where(
            (lane & dist) == 0, a + pltpu.roll(a, 128 - dist, 1), b + pltpu.roll(b, dist, 1)
        )

    y = over_lanes(0, 5)
    return y + pltpu.roll(y, 96, 1)


def lane_order():
    src = lax.broadcasted_iota(jnp.int32, (128, 128), 0)
    dst = lane_ids((128, 128))
    want = (dst & 1) * 64 + ((dst & 63) >> 1)
    return jnp.where(src == want, 1.0, 0.0).astype(bf16)


def reorder(y, perm):
    return fold(mm(pieces(y), perm))


def pack_rows(y):
    return jnp.where(lane_ids((4, 128)) < 64, y[:4], y[4:])


def unpack_rows(v):
    turned = pltpu.roll(v, 64, 1)
    low = lane_ids((4, 128)) < 64
    return jnp.concatenate([jnp.where(low, v, turned), jnp.where(low, turned, v)], axis=0)


def one_hot(order_row):
    rows = lax.broadcasted_iota(jnp.int32, (POINTS, POINTS), 0)
    return jnp.where(rows == order_row, 1.0, 0.0).astype(bf16)


CHUNK = 8
ROUNDS_A = 7
ROUNDS_B = 8


def three(raw):
    high = raw.astype(bf16).astype(f32)
    rest = raw - high
    mid = rest.astype(bf16).astype(f32)
    return high, mid, rest - mid


def unit_rows():
    rows = lax.broadcasted_iota(jnp.int32, (4, POINTS), 0)
    return rows, jnp.where(rows == 0, 1.0, 0.0)


def source_features(geo):
    h, m, t = three(jnp.concatenate([geo, unit_rows()[1]], axis=0))
    zero = jnp.zeros_like(h)
    return jnp.concatenate([h, m, t, h, m, h, zero, zero], axis=0).T.astype(bf16)


def target_features(geo):
    rows, _ = unit_rows()
    turned = jnp.where(rows < 3, geo * -2.0, 1.0)
    low = jnp.where(rows == 0, geo[3:4, :], 0.0)
    h, m, t = three(jnp.concatenate([turned, low], axis=0))
    zero = jnp.zeros_like(h)
    return jnp.concatenate([h, h, h, m, m, t, zero, zero], axis=0).astype(bf16)


def up_kernel(
    device_ref, near_list_in, near_count_in, probes_in, coords_in, order_in, basis_in, transfer_in,
    halo, coef, lists, counts, feat, target, s16_out,
    dup, transfer, probes, coords, order, basis, near_list, near_count, sems, few,
):
    chunks = LEAVES // CHUNK
    small = [
        pltpu.make_async_copy(src, dst, few.at[i])
        for i, (src, dst) in enumerate(
            ((near_list_in, near_list), (near_count_in, near_count), (transfer_in, transfer))
        )
    ]
    loads = []
    for j in range(chunks):
        part = pl.ds(j * CHUNK, CHUNK)
        pairs = (
            (probes_in.at[part], probes.at[part]),
            (coords_in.at[:, part], coords.at[:, part]),
            (order_in.at[part], order.at[part]),
            (basis_in.at[part], basis.at[part]),
        )
        loads.append(
            [pltpu.make_async_copy(src, dst, sems.at[j, i]) for i, (src, dst) in enumerate(pairs)]
        )
    for copy in small[:2] + [copy for chunk in loads for copy in chunk] + small[2:]:
        copy.start()
    target[LEAVES] = jnp.zeros_like(target[LEAVES])
    base = (device_ref[0] - 1) * LEAVES

    def leaf(l, filled):
        p16 = pieces(probes[l])
        s16 = mm(p16, one_hot(order[pl.ds(l, 1), :]))
        xyz = jnp.concatenate([coords[c, pl.ds(l, 1), :] for c in range(3)], axis=0)
        xyz = (xyz - 0.5) * COORD_SCALE
        geo = jnp.concatenate([xyz, jnp.sum(xyz * xyz, axis=0, keepdims=True)], axis=0)
        halo[l] = jnp.concatenate([fold(s16), geo], axis=0)
        feat[l] = source_features(geo)
        target[l] = target_features(geo)
        s16 = s16.astype(bf16)
        s16_out[l] = s16
        high, low = split2(basis[l])
        c = fold(mm_nt(s16, high) + mm_nt(s16, low))
        c = jnp.concatenate([c, c], axis=1)
        dup[pl.ds(pl.multiple_of(l * 8, 8), 8), :] = c
        coef[l] = pack_rows(c)
        filled = list(filled)
        used = near_count[l]
        for k in range(8):
            row = near_list[k, l] - base
            side = lax.shift_right_logical(row, 5)
            here = side == 1
            code = l * 64 + (row & 31) + jnp.where(side == 2, 32, 0)
            for which, fits in enumerate((here, jnp.logical_not(here))):
                at = filled[which]
                lists[which, at] = code
                filled[which] = at + jnp.where(fits & (k < used), 1, 0)
        return tuple(filled)

    filled = (jnp.int32(0), jnp.int32(0))
    for copy in small[:2]:
        copy.wait()
    for j in range(chunks):
        for copy in loads[j]:
            copy.wait()
        filled = lax.fori_loop(j * CHUNK, (j + 1) * CHUNK, leaf, filled, unroll=CHUNK)
    for which in range(2):
        counts[which] = filled[which]
        for pad in range(UNROLL):
            lists[which, filled[which] + pad] = LEAVES * 64
    small[2].wait()
    coefs = [
        [dup[pl.ds(p + 64 * h, 8, stride=8), :] for h in range(4)] for p in range(PROBES)
    ]
    y = contract(
        lambda t, h: transfer[8 * h : 8 * h + 8, 128 * t : 128 * t + 128], coefs, 4
    )
    coef[LEAVES] = pack_rows(reorder(y, lane_order()))


def near_rounds(which, start, stop, lists, feat, target, s16, acc):
    def tiles(step, carry):
        for i in range(UNROLL):
            code = lists[which, step * UNROLL + i]
            l = lax.shift_right_logical(code, 6)
            m = code & 63
            square = jnp.maximum(mm(feat[m], target[l]), 1e-30)
            dist = square * lax.rsqrt(square)
            kern = (LOG2E + dist) * jnp.exp2(-dist)
            high, low = split2(kern)
            s = s16[m]
            acc[l] += mm(s, high) + mm(s, low)
        return carry

    lax.fori_loop(start, stop, tiles, 0)


def near_plan(counts):
    own = (counts[0] + UNROLL - 1) // UNROLL
    far = (counts[1] + UNROLL - 1) // UNROLL
    cut = jnp.minimum(own, ROUNDS_A)
    turn = jnp.minimum(far, jnp.maximum(ROUNDS_B - (own - cut), 0))
    return own, cut, turn, far


def near_finish(acc, out):
    for l in range(LEAVES):
        out[l] = fold(acc[l]) * (AMPLITUDE / LOG2E)


def near_a_kernel(lists, counts, feat, target, s16, out, acc):
    acc[...] = jnp.zeros_like(acc)
    _, cut, _, _ = near_plan(counts)
    near_rounds(0, 0, cut, lists, feat, target, s16, acc)
    near_finish(acc, out)


def near_b_kernel(
    lists, counts, feat, target, s16, below, above, out, halo_feat, halo_s16, acc
):
    acc[...] = jnp.zeros_like(acc)
    own, cut, turn, _ = near_plan(counts)
    near_rounds(0, cut, own, lists, feat, target, s16, acc)
    for side, src in enumerate((below, above)):

        def prepare(l, carry):
            halo_s16[side * LEAVES + l] = pieces(src[l, :8, :])
            halo_feat[side * LEAVES + l] = source_features(src[l, 8:12, :])
            return carry

        lax.fori_loop(0, LEAVES, prepare, 0, unroll=16)
    near_rounds(1, 0, turn, lists, halo_feat, target, halo_s16, acc)
    near_finish(acc, out)


def near_c_kernel(lists, counts, feat, target, s16, out, acc):
    acc[...] = jnp.zeros_like(acc)
    _, _, turn, far = near_plan(counts)
    near_rounds(1, turn, far, lists, feat, target, s16, acc)
    near_finish(acc, out)


FAR_STEP = 8
FAR_UNROLL = 8
HELD = LEAVES + 1
EMPTY = 32 * HELD


def far_kernel(
    device_ref, far_list, far_count, node_list, node_count, coupling, own_side, other_side,
    out, node_rows, table, picked, y_all, lists, used, nodes, sems,
):
    step = pl.program_id(0)
    size = own_side.shape[0]
    copies = [
        pltpu.make_async_copy(src, dst, sems.at[i])
        for i, (src, dst) in enumerate((
            (own_side, table.at[pl.ds(0, size)]),
            (other_side, table.at[pl.ds(size, size)]),
            (far_list, lists),
            (far_count, used),
            (node_list, nodes),
        ))
    ]

    @pl.when(step == 0)
    def _():
        for copy in copies:
            copy.start()
        table[EMPTY] = jnp.zeros((4, 128), f32)
        for copy in copies:
            copy.wait()

    device = device_ref[0]
    grp = lax.shift_right_logical(device, 5)

    def slot_of(block):
        y = (lax.shift_right_logical(block, 3) - lax.shift_right_logical(device, 3)) & 3
        x = (lax.shift_right_logical(block, 1) - lax.shift_right_logical(device, 1)) & 3
        return ((block ^ device) & 1) * 16 + y * 4 + x

    low = lane_ids((4, 128)) < 64

    def leaf(i, carry):
        l = step * FAR_STEP + i
        at = pl.multiple_of(i * 256, 256)
        for k in range(16):
            local = lists[k, l] - grp * 1024
            slot = slot_of(lax.shift_right_logical(local, 5))
            row = jnp.where(k < used[l], slot * HELD + (local & 31), EMPTY)
            held = table[row]
            turned = pltpu.roll(held, 64, 1)
            for j, (left, right) in enumerate(((held, 0.0), (turned, 0.0), (0.0, turned), (0.0, held))):
                picked[pl.ds(at + k * 16 + 4 * j, 4), :] = jnp.where(low, left, right)
        coefs = jnp.concatenate([picked[pl.ds(at + k * 16, 16), :] for k in range(16)], axis=1)
        blocks = []
        for k in range(16):
            base = pl.multiple_of((i * 2 + k // 8) * 256, 256) + k % 8
            blocks.append(coupling[pl.ds(base, 32, stride=8), :])
        high, lower = split2(jnp.concatenate(blocks, axis=1))
        c16 = pieces(coefs)
        y = fold(mm_nt(c16, high) + mm_nt(c16, lower))
        gap = jnp.zeros((8, 32), f32)
        y_all[pl.ds(pl.multiple_of(l * 16, 16), 16), :] = pieces(
            jnp.concatenate([y[:8], gap, y[8:], gap], axis=1)
        )
        return carry

    lax.fori_loop(0, FAR_STEP, leaf, 0, unroll=FAR_UNROLL)

    @pl.when(step == LEAVES // FAR_STEP - 1)
    def _():
        y = mm(y_all[...], lane_order()).reshape(LEAVES, 2, 8, 128)
        out[...] = y[:, 0] + y[:, 1]
        for k in range(8):
            node = nodes[0, k]
            turn = (lax.shift_right_logical(node, 5) - grp) & 3
            node_rows[k] = jnp.where(k < node_count[0], turn * 32 + slot_of(node & 31), 128)


def down_kernel(
    node_rows, nodes0, nodes1, nodes2, nodes3, node_coupling, transfer, basis, order, far,
    near_a, near_b, near_c, out, table, picked, wide, from_node,
):
    for g, nodes in enumerate((nodes0, nodes1, nodes2, nodes3)):
        table[32 * g : 32 * g + 32] = nodes[...]
    table[128] = jnp.zeros((4, 128), f32)
    for k in range(8):
        picked[pl.ds(k * 8, 8), :] = unpack_rows(table[node_rows[k]])
    coefs = [[picked[pl.ds(p, 8, stride=8), :]] for p in range(PROBES)]
    y = contract(lambda t, h: node_coupling[0, :, 128 * t : 128 * t + 128], coefs, 1)
    low = lane_ids((8, 128)) < 64
    for t in range(32):
        wide[:, 128 * t : 128 * t + 128] = jnp.where(low, y[:, t : t + 1], y[:, 64 + t : 65 + t])
    for p in range(PROBES):
        totals = [jnp.zeros((8, 128), f32)] * 4
        for t in range(32):
            factor = wide[p : p + 1, 128 * t : 128 * t + 128]
            for h in range(4):
                totals[h] += transfer[8 * h : 8 * h + 8, 128 * t : 128 * t + 128] * factor
        for h in range(4):
            from_node[pl.ds(p + 64 * h, 8, stride=8), :] = totals[h] + pltpu.roll(totals[h], 64, 1)

    def leaf(l, carry):
        near = near_a[l] + near_b[l] + near_c[l]
        leaf_out = (
            far[l] + from_node[pl.ds(pl.multiple_of(l * 8, 8), 8), :]
        )[:, :RANK]
        high, lower = split2(basis[l])
        leaf16 = pieces(leaf_out)
        total = fold(mm(leaf16, high) + mm(leaf16, lower)) + near
        out[l] = fold(mm_nt(pieces(total), one_hot(order[pl.ds(l, 1), :])))
        return carry

    lax.fori_loop(0, LEAVES, leaf, 0, unroll=16)


VM = pl.BlockSpec(memory_space=pltpu.VMEM)
SM = pl.BlockSpec(memory_space=pltpu.SMEM)
ANY = pl.BlockSpec(memory_space=pl.ANY)


HBM = pl.BlockSpec(memory_space=pltpu.HBM)


def near_call(kernel, extra, name, *args):
    return pl.pallas_call(
        kernel,
        out_shape=(jax.ShapeDtypeStruct((LEAVES, PROBES, POINTS), f32), *extra),
        in_specs=[SM, SM] + [VM] * (len(args) - 2),
        out_specs=(VM,) * (1 + len(extra)),
        scratch_shapes=[pltpu.VMEM((LEAVES + 1, 16, POINTS), f32)],
        compiler_params=pltpu.CompilerParams(vmem_limit_bytes=BIG),
        cost_estimate=pl.CostEstimate(
            flops=12 * 10**9, bytes_accessed=30 * 10**6, transcendentals=8 * 10**6
        ),
        name=name,
    )(*args)


def body(
    probes, coords, order, basis, transfer, far_list, far_count, far_coupling, node_list,
    node_count, node_coupling, near_list, near_count,
):
    grp, leaf = lax.axis_index("grp"), lax.axis_index("leaf")
    groups, blocks = lax.axis_size("grp"), lax.axis_size("leaf")
    device = (grp * blocks + leaf).reshape(1).astype(jnp.int32)
    some = lambda *shape: jax.ShapeDtypeStruct(shape, f32)
    ints = lambda *shape: jax.ShapeDtypeStruct(shape, jnp.int32)
    short = lambda *shape: jax.ShapeDtypeStruct(shape, bf16)

    halo, coef, lists, counts, feat, target, s16 = pl.pallas_call(
        up_kernel,
        out_shape=(
            some(LEAVES, 12, POINTS), some(HELD, 4, 128), ints(2, TILE_SLOTS), ints(2),
            short(LEAVES, POINTS, 64), short(LEAVES + 1, 64, POINTS), short(LEAVES, 16, POINTS),
        ),
        in_specs=[SM] + [HBM] * 7,
        out_specs=(VM, VM, SM, SM, VM, VM, VM),
        scratch_shapes=[
            pltpu.VMEM((LEAVES * 8, 128), f32),
            pltpu.VMEM((LEAVES, RANK * RANK), f32),
            pltpu.VMEM((LEAVES, PROBES, POINTS), f32),
            pltpu.VMEM((3, LEAVES, POINTS), f32),
            pltpu.VMEM((LEAVES, POINTS), jnp.int32),
            pltpu.VMEM((LEAVES, RANK, POINTS), f32),
            pltpu.SMEM((8, LEAVES), jnp.int32),
            pltpu.SMEM((LEAVES,), jnp.int32),
            pltpu.SemaphoreType.DMA((LEAVES // CHUNK, 4)),
            pltpu.SemaphoreType.DMA((3,)),
        ],
        compiler_params=pltpu.CompilerParams(vmem_limit_bytes=BIG),
        name="up",
    )(
        device,
        *(
            pltpu.with_memory_space_constraint(array, pltpu.HBM)
            for array in (
                near_list.T, near_count, probes, coords.transpose(1, 0, 2), order, basis, transfer
            )
        ),
    )

    below = lax.ppermute(halo, "leaf", [(i, (i + 1) % blocks) for i in range(blocks)])
    above = lax.ppermute(halo, "leaf", [((i + 1) % blocks, i) for i in range(blocks)])

    def place(y, x, c):
        return ((y % 4) * 4 + x % 4) * 2 + c

    everyone = [(y, x, c) for y in range(4) for x in range(4) for c in range(2)]

    def shift(part, dy, dx, dc):
        pairs = [(place(y + dy, x + dx, c ^ dc), place(y, x, c)) for y, x, c in everyone]
        return lax.ppermute(part, "leaf", pairs)

    along_x = [coef] + [shift(coef, 0, i, 0) for i in range(1, 4)]
    near_a = near_call(near_a_kernel, (), "near_a", lists, counts, feat, target, s16)[0]
    *along_x, near_a, below, above = lax.optimization_barrier((*along_x, near_a, below, above))
    line = jnp.concatenate(along_x, axis=0)
    line, lists_b = lax.optimization_barrier((line, lists))
    planes = [line] + [shift(line, i, 0, 0) for i in range(1, 4)]
    near_b, halo_feat, halo_s16 = near_call(
        near_b_kernel,
        (short(2 * LEAVES, POINTS, 64), short(2 * LEAVES, 16, POINTS)),
        "near_b", lists_b, counts, feat, target, s16, below, above,
    )
    *planes, near_b = lax.optimization_barrier((*planes, near_b))
    own_side = jnp.concatenate(planes, axis=0)
    own_side, lists_c = lax.optimization_barrier((own_side, lists_b))
    other_side = shift(own_side, 0, 0, 1)
    near_c = near_call(
        near_c_kernel, (), "near_c", lists_c, counts, halo_feat, target, halo_s16
    )[0]
    other_side, near_c = lax.optimization_barrier((other_side, near_c))
    nodes = jnp.concatenate(
        [part.reshape(16, HELD, 4, 128)[:, LEAVES] for part in (own_side, other_side)], axis=0
    )
    all_nodes = [nodes] + [
        lax.ppermute(nodes, "grp", [((g + i) % groups, g) for g in range(groups)])
        for i in range(1, groups)
    ]

    lying = far_coupling.reshape(LEAVES, 2, 8, 32, 128).transpose(0, 1, 3, 2, 4).reshape(-1, 128)
    far, node_rows = pl.pallas_call(
        far_kernel,
        grid=(LEAVES // FAR_STEP,),
        out_shape=(some(LEAVES, 8, 128), ints(8)),
        in_specs=[SM, ANY, ANY, ANY, SM, pl.BlockSpec((FAR_STEP * 512, 128), lambda i: (i, 0)), ANY, ANY],
        out_specs=(VM, SM),
        scratch_shapes=[
            pltpu.VMEM((EMPTY + 1, 4, 128), f32),
            pltpu.VMEM((FAR_STEP * 256, 128), f32),
            pltpu.VMEM((LEAVES * 16, 128), bf16),
            pltpu.SMEM((16, LEAVES), jnp.int32),
            pltpu.SMEM((LEAVES,), jnp.int32),
            pltpu.SMEM((1, 8), jnp.int32),
            pltpu.SemaphoreType.DMA((5,)),
        ],
        compiler_params=pltpu.CompilerParams(vmem_limit_bytes=BIG),
        cost_estimate=pl.CostEstimate(
            flops=12 * 10**9, bytes_accessed=20 * 10**6, transcendentals=0
        ),
        name="far",
    )(
        device,
        *(
            pltpu.with_memory_space_constraint(array, pltpu.HBM)
            for array in (far_list.T, far_count, node_list)
        ),
        node_count,
        lying, own_side, other_side,
    )

    return pl.pallas_call(
        down_kernel,
        out_shape=some(LEAVES, PROBES, POINTS),
        in_specs=[SM] + [VM] * 12,
        out_specs=VM,
        scratch_shapes=[
            pltpu.VMEM((129, 4, 128), f32),
            pltpu.VMEM((64, 128), f32),
            pltpu.VMEM((8, RANK * RANK), f32),
            pltpu.VMEM((LEAVES * 8, 128), f32),
        ],
        compiler_params=pltpu.CompilerParams(vmem_limit_bytes=BIG),
        name="down",
    )(
        node_rows, *all_nodes, node_coupling, transfer, basis, order, far, near_a, near_b, near_c
    )


def solution(mesh):
    rows = ("grp", "leaf")
    return jax.shard_map(
        body,
        mesh=mesh,
        in_specs=(
            P(rows, None, None), P(rows, None, None), P(rows, None), P(rows, None, None),
            P(rows, None), P(rows, None), P(rows), P(rows, None, None), P(rows, None), P(rows),
            P(rows, None, None), P(rows, None), P(rows),
        ),
        out_specs=P(rows, None, None),
        check_vma=False,
    )
```

```python
import functools
import math

import jax
import jax.numpy as jnp
from jax import lax
from jax.experimental import pallas as pl
from jax.experimental.pallas import tpu as pltpu
from jax.sharding import PartitionSpec as P

f32 = jnp.float32
bf16 = jnp.bfloat16
LOG2E = 1.0 / math.log(2.0)
AMPLITUDE = 0.0625
COORD_SCALE = math.sqrt(3.0) / 0.15 * LOG2E
LEAVES = 32
PROBES = 8
POINTS = 256
RANK = 64
UNROLL = 8
TILE_SLOTS = 264
BIG = 20 * 2**20

NT = (((1,), (1,)), ((), ()))


def split2(x):
    high = x.astype(bf16)
    return high, (x - high.astype(f32)).astype(bf16)


def pieces(x):
    high, low = split2(x)
    return jnp.concatenate([high, low], axis=0)


def fold(x):
    half = x.shape[0] // 2
    return x[:half] + x[half:]


def mm(a, b):
    return jnp.dot(a, b, preferred_element_type=f32)


def mm_nt(a, b):
    return lax.dot_general(a, b, NT, preferred_element_type=f32)


def lane_ids(shape):
    return lax.broadcasted_iota(jnp.int32, shape, len(shape) - 1)


def contract(tile, coefs, steps):
    sub = lax.broadcasted_iota(jnp.int32, (8, 128), 0)
    lane = lane_ids((8, 128))

    def over_slots(t):
        blocks = [tile(t, h) for h in range(steps)]
        vs = []
        for p in range(PROBES):
            total = blocks[0] * coefs[p][0]
            for h in range(1, steps):
                total = total + blocks[h] * coefs[p][h]
            vs.append(total)
        for dist in (1, 2, 4):
            keep = (sub & dist) == 0
            vs = [
                jnp.where(keep, a, b) + pltpu.roll(jnp.where(keep, b, a), dist, 0)
                for a, b in zip(vs[0::2], vs[1::2])
            ]
        return vs[0]

    def over_lanes(t0, bits):
        if bits == 0:
            return over_slots(t0)
        dist = 1 << (bits - 1)
        a = over_lanes(t0, bits - 1)
        b = over_lanes(t0 + dist, bits - 1)
        return jnp.where(
            (lane & dist) == 0, a + pltpu.roll(a, 128 - dist, 1), b + pltpu.roll(b, dist, 1)
        )

    y = over_lanes(0, 5)
    return y + pltpu.roll(y, 96, 1)


def lane_order():
    src = lax.broadcasted_iota(jnp.int32, (128, 128), 0)
    dst = lane_ids((128, 128))
    want = (dst & 1) * 64 + ((dst & 63) >> 1)
    return jnp.where(src == want, 1.0, 0.0).astype(bf16)


def reorder(y, perm):
    return fold(mm(pieces(y), perm))


def pack_rows(y):
    return jnp.where(lane_ids((4, 128)) < 64, y[:4], y[4:])


def unpack_rows(v):
    turned = pltpu.roll(v, 64, 1)
    low = lane_ids((4, 128)) < 64
    return jnp.concatenate([jnp.where(low, v, turned), jnp.where(low, turned, v)], axis=0)


def one_hot(order_row):
    rows = lax.broadcasted_iota(jnp.int32, (POINTS, POINTS), 0)
    return jnp.where(rows == order_row, 1.0, 0.0).astype(bf16)


CHUNK = 8
ROUNDS_A = 5
ROUNDS_B = 10


def three(raw):
    high = raw.astype(bf16).astype(f32)
    rest = raw - high
    mid = rest.astype(bf16).astype(f32)
    return high, mid, rest - mid


def unit_rows():
    rows = lax.broadcasted_iota(jnp.int32, (4, POINTS), 0)
    return rows, jnp.where(rows == 0, 1.0, 0.0)


def source_features(geo):
    h, m, t = three(jnp.concatenate([geo, unit_rows()[1]], axis=0))
    zero = jnp.zeros_like(h)
    return jnp.concatenate([h, m, t, h, m, h, zero, zero], axis=0).T.astype(bf16)


def target_features(geo):
    rows, _ = unit_rows()
    turned = jnp.where(rows < 3, geo * -2.0, 1.0)
    low = jnp.where(rows == 0, geo[3:4, :], 0.0)
    h, m, t = three(jnp.concatenate([turned, low], axis=0))
    zero = jnp.zeros_like(h)
    return jnp.concatenate([h, h, h, m, m, t, zero, zero], axis=0).astype(bf16)


def up_kernel(
    device_ref, near_list_in, near_count_in, probes_in, coords_in, order_in, basis_in, transfer_in,
    halo, coef, lists, counts, feat, target, s16_out,
    dup, transfer, probes, coords, order, basis, near_list, near_count, sems, few,
):
    chunks = LEAVES // CHUNK
    small = [
        pltpu.make_async_copy(src, dst, few.at[i])
        for i, (src, dst) in enumerate(
            ((near_list_in, near_list), (near_count_in, near_count), (transfer_in, transfer))
        )
    ]
    loads = []
    for j in range(chunks):
        part = pl.ds(j * CHUNK, CHUNK)
        pairs = (
            (probes_in.at[part], probes.at[part]),
            (coords_in.at[:, part], coords.at[:, part]),
            (order_in.at[part], order.at[part]),
            (basis_in.at[part], basis.at[part]),
        )
        loads.append(
            [pltpu.make_async_copy(src, dst, sems.at[j, i]) for i, (src, dst) in enumerate(pairs)]
        )
    for copy in small[:2] + [copy for chunk in loads for copy in chunk] + small[2:]:
        copy.start()
    target[LEAVES] = jnp.zeros_like(target[LEAVES])
    base = (device_ref[0] - 1) * LEAVES

    def leaf(l, filled):
        p16 = pieces(probes[l])
        s16 = mm(p16, one_hot(order[pl.ds(l, 1), :]))
        xyz = jnp.concatenate([coords[c, pl.ds(l, 1), :] for c in range(3)], axis=0)
        xyz = (xyz - 0.5) * COORD_SCALE
        geo = jnp.concatenate([xyz, jnp.sum(xyz * xyz, axis=0, keepdims=True)], axis=0)
        halo[l] = jnp.concatenate([fold(s16), geo], axis=0)
        feat[l] = source_features(geo)
        target[l] = target_features(geo)
        s16 = s16.astype(bf16)
        s16_out[l] = s16
        high, low = split2(basis[l])
        c = fold(mm_nt(s16, high) + mm_nt(s16, low))
        c = jnp.concatenate([c, c], axis=1)
        dup[pl.ds(pl.multiple_of(l * 8, 8), 8), :] = c
        coef[l] = pack_rows(c)
        filled = list(filled)
        used = near_count[l]
        for k in range(8):
            row = near_list[k, l] - base
            side = lax.shift_right_logical(row, 5)
            here = side == 1
            code = l * 64 + (row & 31) + jnp.where(side == 2, 32, 0)
            for which, fits in enumerate((here, jnp.logical_not(here))):
                at = filled[which]
                lists[which, at] = code
                filled[which] = at + jnp.where(fits & (k < used), 1, 0)
        return tuple(filled)

    filled = (jnp.int32(0), jnp.int32(0))
    for copy in small[:2]:
        copy.wait()
    for j in range(chunks):
        for copy in loads[j]:
            copy.wait()
        filled = lax.fori_loop(j * CHUNK, (j + 1) * CHUNK, leaf, filled, unroll=CHUNK)
    for which in range(2):
        counts[which] = filled[which]
        for pad in range(UNROLL):
            lists[which, filled[which] + pad] = LEAVES * 64
    small[2].wait()
    coefs = [
        [dup[pl.ds(p + 64 * h, 8, stride=8), :] for h in range(4)] for p in range(PROBES)
    ]
    y = contract(
        lambda t, h: transfer[8 * h : 8 * h + 8, 128 * t : 128 * t + 128], coefs, 4
    )
    coef[LEAVES] = pack_rows(reorder(y, lane_order()))


def near_rounds(which, start, stop, lists, feat, target, s16, acc):
    def tiles(step, carry):
        for i in range(UNROLL):
            code = lists[which, step * UNROLL + i]
            l = lax.shift_right_logical(code, 6)
            m = code & 63
            square = jnp.maximum(mm(feat[m], target[l]), 1e-30)
            dist = square * lax.rsqrt(square)
            kern = (LOG2E + dist) * jnp.exp2(-dist)
            high, low = split2(kern)
            s = s16[m]
            acc[l] += mm(s, high) + mm(s, low)
        return carry

    lax.fori_loop(start, stop, tiles, 0)


def near_plan(counts):
    own = (counts[0] + UNROLL - 1) // UNROLL
    far = (counts[1] + UNROLL - 1) // UNROLL
    cut = jnp.minimum(own, ROUNDS_A)
    turn = jnp.minimum(far, jnp.maximum(ROUNDS_B - (own - cut), 0))
    return own, cut, turn, far


def near_finish(acc, out):
    for l in range(LEAVES):
        out[l] = fold(acc[l]) * (AMPLITUDE / LOG2E)


def near_a_kernel(lists, counts, feat, target, s16, out, acc):
    acc[...] = jnp.zeros_like(acc)
    _, cut, _, _ = near_plan(counts)
    near_rounds(0, 0, cut, lists, feat, target, s16, acc)
    near_finish(acc, out)


def near_b_kernel(
    lists, counts, feat, target, s16, below, above, out, halo_feat, halo_s16, acc
):
    acc[...] = jnp.zeros_like(acc)
    own, cut, turn, _ = near_plan(counts)
    near_rounds(0, cut, own, lists, feat, target, s16, acc)
    for side, src in enumerate((below, above)):

        def prepare(l, carry):
            halo_s16[side * LEAVES + l] = pieces(src[l, :8, :])
            halo_feat[side * LEAVES + l] = source_features(src[l, 8:12, :])
            return carry

        lax.fori_loop(0, LEAVES, prepare, 0, unroll=16)
    near_rounds(1, 0, turn, lists, halo_feat, target, halo_s16, acc)
    near_finish(acc, out)


def near_c_kernel(lists, counts, feat, target, s16, out, acc):
    acc[...] = jnp.zeros_like(acc)
    _, _, turn, far = near_plan(counts)
    near_rounds(1, turn, far, lists, feat, target, s16, acc)
    near_finish(acc, out)


FAR_CHUNK = 8
HELD = LEAVES + 1


def far_kernel(
    device_ref, far_list, far_count, node_list, node_count, coupling, own_side, other_side,
    out, node_rows, picked, y_all, lists, used, nodes, sems,
):
    copies = [
        pltpu.make_async_copy(src, dst, sems.at[i])
        for i, (src, dst) in enumerate(((far_list, lists), (far_count, used), (node_list, nodes)))
    ]
    for copy in copies:
        copy.start()
    for copy in copies:
        copy.wait()

    device = device_ref[0]
    grp = lax.shift_right_logical(device, 5)

    def slot_of(block):
        y = (lax.shift_right_logical(block, 3) - lax.shift_right_logical(device, 3)) & 3
        x = (lax.shift_right_logical(block, 1) - lax.shift_right_logical(device, 1)) & 3
        return ((block ^ device) & 1) * 16 + y * 4 + x

    low = lane_ids((4, 128)) < 64

    def leaf(chunk, i):
        l = chunk * FAR_CHUNK + i
        at = i * 256
        for k in range(16):
            local = lists[k, l] - grp * 1024
            slot = slot_of(lax.shift_right_logical(local, 5))
            row = (slot & 15) * HELD + (local & 31)
            held = jnp.where(slot < 16, own_side[row], other_side[row])
            held = jnp.where(k < used[l], held, 0.0)
            turned = pltpu.roll(held, 64, 1)
            for j, (left, right) in enumerate(((held, 0.0), (turned, 0.0), (0.0, turned), (0.0, held))):
                picked[pl.ds(at + k * 16 + 4 * j, 4), :] = jnp.where(low, left, right)
        coefs = jnp.concatenate([picked[pl.ds(at + k * 16, 16), :] for k in range(16)], axis=1)
        blocks = []
        for k in range(16):
            base = pl.multiple_of((l * 2 + k // 8) * 256, 256) + k % 8
            blocks.append(coupling[pl.ds(base, 32, stride=8), :])
        high, lower = split2(jnp.concatenate(blocks, axis=1))
        c16 = pieces(coefs)
        y = fold(mm_nt(c16, high) + mm_nt(c16, lower))
        gap = jnp.zeros((8, 32), f32)
        y_all[pl.ds(pl.multiple_of(l * 16, 16), 16), :] = pieces(
            jnp.concatenate([y[:8], gap, y[8:], gap], axis=1)
        )

    def chunk_of_leaves(chunk, carry):
        for i in range(FAR_CHUNK):
            leaf(chunk, i)
        return carry

    lax.fori_loop(0, LEAVES // FAR_CHUNK, chunk_of_leaves, 0)
    y = mm(y_all[...], lane_order()).reshape(LEAVES, 2, 8, 128)
    out[...] = y[:, 0] + y[:, 1]
    for k in range(8):
        node = nodes[0, k]
        turn = (lax.shift_right_logical(node, 5) - grp) & 3
        node_rows[k] = jnp.where(k < node_count[0], turn * 32 + slot_of(node & 31), 128)


def down_kernel(
    node_rows, nodes0, nodes1, nodes2, nodes3, node_coupling, transfer, basis, order, far,
    near_a, near_b, near_c, out, table, picked, wide, from_node,
):
    for g, nodes in enumerate((nodes0, nodes1, nodes2, nodes3)):
        table[32 * g : 32 * g + 32] = nodes[...]
    table[128] = jnp.zeros((4, 128), f32)
    for k in range(8):
        picked[pl.ds(k * 8, 8), :] = unpack_rows(table[node_rows[k]])
    coefs = [[picked[pl.ds(p, 8, stride=8), :]] for p in range(PROBES)]
    y = contract(lambda t, h: node_coupling[0, :, 128 * t : 128 * t + 128], coefs, 1)
    low = lane_ids((8, 128)) < 64
    for t in range(32):
        wide[:, 128 * t : 128 * t + 128] = jnp.where(low, y[:, t : t + 1], y[:, 64 + t : 65 + t])
    for p in range(PROBES):
        totals = [jnp.zeros((8, 128), f32)] * 4
        for t in range(32):
            factor = wide[p : p + 1, 128 * t : 128 * t + 128]
            for h in range(4):
                totals[h] += transfer[8 * h : 8 * h + 8, 128 * t : 128 * t + 128] * factor
        for h in range(4):
            from_node[pl.ds(p + 64 * h, 8, stride=8), :] = totals[h] + pltpu.roll(totals[h], 64, 1)

    def leaf(l, carry):
        near = near_a[l] + near_b[l] + near_c[l]
        leaf_out = (
            far[l] + from_node[pl.ds(pl.multiple_of(l * 8, 8), 8), :]
        )[:, :RANK]
        high, lower = split2(basis[l])
        leaf16 = pieces(leaf_out)
        total = fold(mm(leaf16, high) + mm(leaf16, lower)) + near
        out[l] = fold(mm_nt(pieces(total), one_hot(order[pl.ds(l, 1), :])))
        return carry

    lax.fori_loop(0, LEAVES, leaf, 0, unroll=16)


VM = pl.BlockSpec(memory_space=pltpu.VMEM)
SM = pl.BlockSpec(memory_space=pltpu.SMEM)
ANY = pl.BlockSpec(memory_space=pl.ANY)


HBM = pl.BlockSpec(memory_space=pltpu.HBM)


def near_call(kernel, extra, name, *args):
    return pl.pallas_call(
        kernel,
        out_shape=(jax.ShapeDtypeStruct((LEAVES, PROBES, POINTS), f32), *extra),
        in_specs=[SM, SM] + [VM] * (len(args) - 2),
        out_specs=(VM,) * (1 + len(extra)),
        scratch_shapes=[pltpu.VMEM((LEAVES + 1, 16, POINTS), f32)],
        compiler_params=pltpu.CompilerParams(vmem_limit_bytes=BIG),
        cost_estimate=pl.CostEstimate(
            flops=12 * 10**9, bytes_accessed=30 * 10**6, transcendentals=8 * 10**6
        ),
        name=name,
    )(*args)


def body(
    probes, coords, order, basis, transfer, far_list, far_count, far_coupling, node_list,
    node_count, node_coupling, near_list, near_count,
):
    grp, leaf = lax.axis_index("grp"), lax.axis_index("leaf")
    groups, blocks = lax.axis_size("grp"), lax.axis_size("leaf")
    device = (grp * blocks + leaf).reshape(1).astype(jnp.int32)
    some = lambda *shape: jax.ShapeDtypeStruct(shape, f32)
    ints = lambda *shape: jax.ShapeDtypeStruct(shape, jnp.int32)
    short = lambda *shape: jax.ShapeDtypeStruct(shape, bf16)

    halo, coef, lists, counts, feat, target, s16 = pl.pallas_call(
        up_kernel,
        out_shape=(
            some(LEAVES, 12, POINTS), some(HELD, 4, 128), ints(2, TILE_SLOTS), ints(2),
            short(LEAVES, POINTS, 64), short(LEAVES + 1, 64, POINTS), short(LEAVES, 16, POINTS),
        ),
        in_specs=[SM] + [HBM] * 7,
        out_specs=(VM, VM, SM, SM, VM, VM, VM),
        scratch_shapes=[
            pltpu.VMEM((LEAVES * 8, 128), f32),
            pltpu.VMEM((LEAVES, RANK * RANK), f32),
            pltpu.VMEM((LEAVES, PROBES, POINTS), f32),
            pltpu.VMEM((3, LEAVES, POINTS), f32),
            pltpu.VMEM((LEAVES, POINTS), jnp.int32),
            pltpu.VMEM((LEAVES, RANK, POINTS), f32),
            pltpu.SMEM((8, LEAVES), jnp.int32),
            pltpu.SMEM((LEAVES,), jnp.int32),
            pltpu.SemaphoreType.DMA((LEAVES // CHUNK, 4)),
            pltpu.SemaphoreType.DMA((3,)),
        ],
        compiler_params=pltpu.CompilerParams(vmem_limit_bytes=BIG),
        name="up",
    )(
        device,
        *(
            pltpu.with_memory_space_constraint(array, pltpu.HBM)
            for array in (
                near_list.T, near_count, probes, coords.transpose(1, 0, 2), order, basis, transfer
            )
        ),
    )

    below = lax.ppermute(halo, "leaf", [(i, (i + 1) % blocks) for i in range(blocks)])
    above = lax.ppermute(halo, "leaf", [((i + 1) % blocks, i) for i in range(blocks)])

    def place(y, x, c):
        return ((y % 4) * 4 + x % 4) * 2 + c

    everyone = [(y, x, c) for y in range(4) for x in range(4) for c in range(2)]

    def shift(part, dy, dx, dc):
        pairs = [(place(y + dy, x + dx, c ^ dc), place(y, x, c)) for y, x, c in everyone]
        return lax.ppermute(part, "leaf", pairs)

    along_x = [coef] + [shift(coef, 0, i, 0) for i in range(1, 4)]
    near_a = near_call(near_a_kernel, (), "near_a", lists, counts, feat, target, s16)[0]
    *along_x, near_a, below, above = lax.optimization_barrier((*along_x, near_a, below, above))
    line = jnp.concatenate(along_x, axis=0)
    line, lists_b = lax.optimization_barrier((line, lists))
    planes = [line] + [shift(line, i, 0, 0) for i in range(1, 4)]
    near_b, halo_feat, halo_s16 = near_call(
        near_b_kernel,
        (short(2 * LEAVES, POINTS, 64), short(2 * LEAVES, 16, POINTS)),
        "near_b", lists_b, counts, feat, target, s16, below, above,
    )
    *planes, near_b = lax.optimization_barrier((*planes, near_b))
    own_side = jnp.concatenate(planes, axis=0)
    own_side, lists_c = lax.optimization_barrier((own_side, lists_b))
    other_side = shift(own_side, 0, 0, 1)
    near_c = near_call(
        near_c_kernel, (), "near_c", lists_c, counts, halo_feat, target, halo_s16
    )[0]
    other_side, near_c = lax.optimization_barrier((other_side, near_c))
    nodes = jnp.concatenate(
        [part.reshape(16, HELD, 4, 128)[:, LEAVES] for part in (own_side, other_side)], axis=0
    )
    all_nodes = [nodes] + [
        lax.ppermute(nodes, "grp", [((g + i) % groups, g) for g in range(groups)])
        for i in range(1, groups)
    ]

    lying = far_coupling.reshape(LEAVES, 2, 8, 32, 128).transpose(0, 1, 3, 2, 4).reshape(-1, 128)
    far, node_rows = pl.pallas_call(
        far_kernel,
        out_shape=(some(LEAVES, 8, 128), ints(8)),
        in_specs=[SM, ANY, ANY, ANY, SM, VM, VM, VM],
        out_specs=(VM, SM),
        scratch_shapes=[
            pltpu.VMEM((FAR_CHUNK * 256, 128), f32),
            pltpu.VMEM((LEAVES * 16, 128), bf16),
            pltpu.SMEM((16, LEAVES), jnp.int32),
            pltpu.SMEM((LEAVES,), jnp.int32),
            pltpu.SMEM((1, 8), jnp.int32),
            pltpu.SemaphoreType.DMA((3,)),
        ],
        compiler_params=pltpu.CompilerParams(vmem_limit_bytes=BIG),
        cost_estimate=pl.CostEstimate(
            flops=12 * 10**9, bytes_accessed=20 * 10**6, transcendentals=0
        ),
        name="far",
    )(
        device,
        *(
            pltpu.with_memory_space_constraint(array, pltpu.HBM)
            for array in (far_list.T, far_count, node_list)
        ),
        node_count,
        lying, own_side, other_side,
    )

    return pl.pallas_call(
        down_kernel,
        out_shape=some(LEAVES, PROBES, POINTS),
        in_specs=[SM] + [VM] * 12,
        out_specs=VM,
        scratch_shapes=[
            pltpu.VMEM((129, 4, 128), f32),
            pltpu.VMEM((64, 128), f32),
            pltpu.VMEM((8, RANK * RANK), f32),
            pltpu.VMEM((LEAVES * 8, 128), f32),
        ],
        compiler_params=pltpu.CompilerParams(vmem_limit_bytes=BIG),
        name="down",
    )(
        node_rows, *all_nodes, node_coupling, transfer, basis, order, far, near_a, near_b, near_c
    )


def solution(mesh):
    rows = ("grp", "leaf")
    return jax.shard_map(
        body,
        mesh=mesh,
        in_specs=(
            P(rows, None, None), P(rows, None, None), P(rows, None), P(rows, None, None),
            P(rows, None), P(rows, None), P(rows), P(rows, None, None), P(rows, None), P(rows),
            P(rows, None, None), P(rows, None), P(rows),
        ),
        out_specs=P(rows, None, None),
        check_vma=False,
    )
```

```python
import functools
import math

import jax
import jax.numpy as jnp
from jax import lax
from jax.experimental import pallas as pl
from jax.experimental.pallas import tpu as pltpu
from jax.sharding import PartitionSpec as P

f32 = jnp.float32
bf16 = jnp.bfloat16
LOG2E = 1.0 / math.log(2.0)
AMPLITUDE = 0.0625
COORD_SCALE = math.sqrt(3.0) / 0.15 * LOG2E
LEAVES = 32
PROBES = 8
POINTS = 256
RANK = 64
UNROLL = 8
TILE_SLOTS = 264
BIG = 20 * 2**20

NT = (((1,), (1,)), ((), ()))


def split2(x):
    high = x.astype(bf16)
    return high, (x - high.astype(f32)).astype(bf16)


def pieces(x):
    high, low = split2(x)
    return jnp.concatenate([high, low], axis=0)


def fold(x):
    half = x.shape[0] // 2
    return x[:half] + x[half:]


def mm(a, b):
    return jnp.dot(a, b, preferred_element_type=f32)


def mm_nt(a, b):
    return lax.dot_general(a, b, NT, preferred_element_type=f32)


def lane_ids(shape):
    return lax.broadcasted_iota(jnp.int32, shape, len(shape) - 1)


def contract(tile, coefs, steps):
    sub = lax.broadcasted_iota(jnp.int32, (8, 128), 0)
    lane = lane_ids((8, 128))

    def over_slots(t):
        blocks = [tile(t, h) for h in range(steps)]
        vs = []
        for p in range(PROBES):
            total = blocks[0] * coefs[p][0]
            for h in range(1, steps):
                total = total + blocks[h] * coefs[p][h]
            vs.append(total)
        for dist in (1, 2, 4):
            keep = (sub & dist) == 0
            vs = [
                jnp.where(keep, a, b) + pltpu.roll(jnp.where(keep, b, a), dist, 0)
                for a, b in zip(vs[0::2], vs[1::2])
            ]
        return vs[0]

    def over_lanes(t0, bits):
        if bits == 0:
            return over_slots(t0)
        dist = 1 << (bits - 1)
        a = over_lanes(t0, bits - 1)
        b = over_lanes(t0 + dist, bits - 1)
        return jnp.where(
            (lane & dist) == 0, a + pltpu.roll(a, 128 - dist, 1), b + pltpu.roll(b, dist, 1)
        )

    y = over_lanes(0, 5)
    return y + pltpu.roll(y, 96, 1)


def lane_order():
    src = lax.broadcasted_iota(jnp.int32, (128, 128), 0)
    dst = lane_ids((128, 128))
    want = (dst & 1) * 64 + ((dst & 63) >> 1)
    return jnp.where(src == want, 1.0, 0.0).astype(bf16)


def reorder(y, perm):
    return fold(mm(pieces(y), perm))


def pack_rows(y):
    return jnp.where(lane_ids((4, 128)) < 64, y[:4], y[4:])


def unpack_rows(v):
    turned = pltpu.roll(v, 64, 1)
    low = lane_ids((4, 128)) < 64
    return jnp.concatenate([jnp.where(low, v, turned), jnp.where(low, turned, v)], axis=0)


def one_hot(order_row):
    rows = lax.broadcasted_iota(jnp.int32, (POINTS, POINTS), 0)
    return jnp.where(rows == order_row, 1.0, 0.0).astype(bf16)


CHUNK = 8
ROUNDS_A = 6
ROUNDS_B = 11


def three(raw):
    high = raw.astype(bf16).astype(f32)
    rest = raw - high
    mid = rest.astype(bf16).astype(f32)
    return high, mid, rest - mid


def unit_rows():
    rows = lax.broadcasted_iota(jnp.int32, (4, POINTS), 0)
    return rows, jnp.where(rows == 0, 1.0, 0.0)


def source_features(geo):
    h, m, t = three(jnp.concatenate([geo, unit_rows()[1]], axis=0))
    zero = jnp.zeros_like(h)
    return jnp.concatenate([h, m, t, h, m, h, zero, zero], axis=0).T.astype(bf16)


def target_features(geo):
    rows, _ = unit_rows()
    turned = jnp.where(rows < 3, geo * -2.0, 1.0)
    low = jnp.where(rows == 0, geo[3:4, :], 0.0)
    h, m, t = three(jnp.concatenate([turned, low], axis=0))
    zero = jnp.zeros_like(h)
    return jnp.concatenate([h, h, h, m, m, t, zero, zero], axis=0).astype(bf16)


def up_kernel(
    device_ref, near_list_in, near_count_in, probes_in, coords_in, order_in, basis_in, transfer_in,
    halo, coef, lists, counts, feat, target, s16_out,
    dup, transfer, probes, coords, order, basis, near_list, near_count, sems, few,
):
    chunks = LEAVES // CHUNK
    small = [
        pltpu.make_async_copy(src, dst, few.at[i])
        for i, (src, dst) in enumerate(
            ((near_list_in, near_list), (near_count_in, near_count), (transfer_in, transfer))
        )
    ]
    loads = []
    for j in range(chunks):
        part = pl.ds(j * CHUNK, CHUNK)
        pairs = (
            (probes_in.at[part], probes.at[part]),
            (coords_in.at[:, part], coords.at[:, part]),
            (order_in.at[part], order.at[part]),
            (basis_in.at[part], basis.at[part]),
        )
        loads.append(
            [pltpu.make_async_copy(src, dst, sems.at[j, i]) for i, (src, dst) in enumerate(pairs)]
        )
    for copy in small[:2] + [copy for chunk in loads for copy in chunk] + small[2:]:
        copy.start()
    target[LEAVES] = jnp.zeros_like(target[LEAVES])
    base = (device_ref[0] - 1) * LEAVES

    def leaf(l, filled):
        p16 = pieces(probes[l])
        s16 = mm(p16, one_hot(order[pl.ds(l, 1), :]))
        xyz = jnp.concatenate([coords[c, pl.ds(l, 1), :] for c in range(3)], axis=0)
        xyz = (xyz - 0.5) * COORD_SCALE
        geo = jnp.concatenate([xyz, jnp.sum(xyz * xyz, axis=0, keepdims=True)], axis=0)
        halo[l] = jnp.concatenate([fold(s16), geo], axis=0)
        feat[l] = source_features(geo)
        target[l] = target_features(geo)
        s16 = s16.astype(bf16)
        s16_out[l] = s16
        high, low = split2(basis[l])
        c = fold(mm_nt(s16, high) + mm_nt(s16, low))
        c = jnp.concatenate([c, c], axis=1)
        dup[pl.ds(pl.multiple_of(l * 8, 8), 8), :] = c
        coef[l] = pack_rows(c)
        filled = list(filled)
        used = near_count[l]
        for k in range(8):
            row = near_list[k, l] - base
            side = lax.shift_right_logical(row, 5)
            here = side == 1
            code = l * 64 + (row & 31) + jnp.where(side == 2, 32, 0)
            for which, fits in enumerate((here, jnp.logical_not(here))):
                at = filled[which]
                lists[which, at] = code
                filled[which] = at + jnp.where(fits & (k < used), 1, 0)
        return tuple(filled)

    filled = (jnp.int32(0), jnp.int32(0))
    for copy in small[:2]:
        copy.wait()
    for j in range(chunks):
        for copy in loads[j]:
            copy.wait()
        filled = lax.fori_loop(j * CHUNK, (j + 1) * CHUNK, leaf, filled, unroll=CHUNK)
    for which in range(2):
        counts[which] = filled[which]
        for pad in range(UNROLL):
            lists[which, filled[which] + pad] = LEAVES * 64
    small[2].wait()
    coefs = [
        [dup[pl.ds(p + 64 * h, 8, stride=8), :] for h in range(4)] for p in range(PROBES)
    ]
    y = contract(
        lambda t, h: transfer[8 * h : 8 * h + 8, 128 * t : 128 * t + 128], coefs, 4
    )
    coef[LEAVES] = pack_rows(reorder(y, lane_order()))


def near_rounds(which, start, stop, lists, feat, target, s16, acc):
    def tiles(step, carry):
        for i in range(UNROLL):
            code = lists[which, step * UNROLL + i]
            l = lax.shift_right_logical(code, 6)
            m = code & 63
            square = jnp.maximum(mm(feat[m], target[l]), 1e-30)
            dist = square * lax.rsqrt(square)
            kern = (LOG2E + dist) * jnp.exp2(-dist)
            high, low = split2(kern)
            s = s16[m]
            acc[l] += mm(s, high) + mm(s, low)
        return carry

    lax.fori_loop(start, stop, tiles, 0)


def near_plan(counts):
    own = (counts[0] + UNROLL - 1) // UNROLL
    far = (counts[1] + UNROLL - 1) // UNROLL
    cut = jnp.minimum(own, ROUNDS_A)
    turn = jnp.minimum(far, jnp.maximum(ROUNDS_B - (own - cut), 0))
    return own, cut, turn, far


def near_finish(acc, out):
    for l in range(LEAVES):
        out[l] = fold(acc[l]) * (AMPLITUDE / LOG2E)


def near_a_kernel(lists, counts, feat, target, s16, out, acc):
    acc[...] = jnp.zeros_like(acc)
    _, cut, _, _ = near_plan(counts)
    near_rounds(0, 0, cut, lists, feat, target, s16, acc)
    near_finish(acc, out)


def near_b_kernel(
    lists, counts, feat, target, s16, below, above, out, halo_feat, halo_s16, acc
):
    acc[...] = jnp.zeros_like(acc)
    own, cut, turn, _ = near_plan(counts)
    near_rounds(0, cut, own, lists, feat, target, s16, acc)
    for side, src in enumerate((below, above)):

        def prepare(l, carry):
            halo_s16[side * LEAVES + l] = pieces(src[l, :8, :])
            halo_feat[side * LEAVES + l] = source_features(src[l, 8:12, :])
            return carry

        lax.fori_loop(0, LEAVES, prepare, 0, unroll=16)
    near_rounds(1, 0, turn, lists, halo_feat, target, halo_s16, acc)
    near_finish(acc, out)


def near_c_kernel(lists, counts, feat, target, s16, out, acc):
    acc[...] = jnp.zeros_like(acc)
    _, _, turn, far = near_plan(counts)
    near_rounds(1, turn, far, lists, feat, target, s16, acc)
    near_finish(acc, out)


FAR_CHUNK = 8
HELD = LEAVES + 1


def far_kernel(
    device_ref, far_list, far_count, node_list, node_count, coupling, own_side, other_side,
    out, node_rows, picked, y_all, lists, used, nodes, sems,
):
    copies = [
        pltpu.make_async_copy(src, dst, sems.at[i])
        for i, (src, dst) in enumerate(((far_list, lists), (far_count, used), (node_list, nodes)))
    ]
    for copy in copies:
        copy.start()
    for copy in copies:
        copy.wait()

    device = device_ref[0]
    grp = lax.shift_right_logical(device, 5)

    def slot_of(block):
        y = (lax.shift_right_logical(block, 3) - lax.shift_right_logical(device, 3)) & 3
        x = (lax.shift_right_logical(block, 1) - lax.shift_right_logical(device, 1)) & 3
        return ((block ^ device) & 1) * 16 + y * 4 + x

    low = lane_ids((4, 128)) < 64

    def leaf(chunk, i):
        l = chunk * FAR_CHUNK + i
        at = i * 256
        for k in range(16):
            local = lists[k, l] - grp * 1024
            slot = slot_of(lax.shift_right_logical(local, 5))
            row = (slot & 15) * HELD + (local & 31)
            held = jnp.where(slot < 16, own_side[row], other_side[row])
            held = jnp.where(k < used[l], held, 0.0)
            turned = pltpu.roll(held, 64, 1)
            for j, (left, right) in enumerate(((held, 0.0), (turned, 0.0), (0.0, turned), (0.0, held))):
                picked[pl.ds(at + k * 16 + 4 * j, 4), :] = jnp.where(low, left, right)
        coefs = jnp.concatenate([picked[pl.ds(at + k * 16, 16), :] for k in range(16)], axis=1)
        blocks = []
        for k in range(16):
            base = pl.multiple_of((l * 2 + k // 8) * 256, 256) + k % 8
            blocks.append(coupling[pl.ds(base, 32, stride=8), :])
        high, lower = split2(jnp.concatenate(blocks, axis=1))
        c16 = pieces(coefs)
        y = fold(fold(mm_nt(jnp.concatenate([high, lower], axis=0), c16)).T)
        gap = jnp.zeros((8, 32), f32)
        y_all[pl.ds(pl.multiple_of(l * 16, 16), 16), :] = pieces(
            jnp.concatenate([y[:8], gap, y[8:], gap], axis=1)
        )

    def chunk_of_leaves(chunk, carry):
        for i in range(FAR_CHUNK):
            leaf(chunk, i)
        return carry

    lax.fori_loop(0, LEAVES // FAR_CHUNK, chunk_of_leaves, 0)
    y = mm(y_all[...], lane_order()).reshape(LEAVES, 2, 8, 128)
    out[...] = y[:, 0] + y[:, 1]
    for k in range(8):
        node = nodes[0, k]
        turn = (lax.shift_right_logical(node, 5) - grp) & 3
        node_rows[k] = jnp.where(k < node_count[0], turn * 32 + slot_of(node & 31), 128)


def down_kernel(
    node_rows, nodes0, nodes1, nodes2, nodes3, node_coupling, transfer, basis, order, far,
    near_a, near_b, near_c, out, table, picked, wide, from_node,
):
    for g, nodes in enumerate((nodes0, nodes1, nodes2, nodes3)):
        table[32 * g : 32 * g + 32] = nodes[...]
    table[128] = jnp.zeros((4, 128), f32)
    for k in range(8):
        picked[pl.ds(k * 8, 8), :] = unpack_rows(table[node_rows[k]])
    coefs = [[picked[pl.ds(p, 8, stride=8), :]] for p in range(PROBES)]
    y = contract(lambda t, h: node_coupling[0, :, 128 * t : 128 * t + 128], coefs, 1)
    low = lane_ids((8, 128)) < 64
    for t in range(32):
        wide[:, 128 * t : 128 * t + 128] = jnp.where(low, y[:, t : t + 1], y[:, 64 + t : 65 + t])
    for p in range(PROBES):
        totals = [jnp.zeros((8, 128), f32)] * 4
        for t in range(32):
            factor = wide[p : p + 1, 128 * t : 128 * t + 128]
            for h in range(4):
                totals[h] += transfer[8 * h : 8 * h + 8, 128 * t : 128 * t + 128] * factor
        for h in range(4):
            from_node[pl.ds(p + 64 * h, 8, stride=8), :] = totals[h] + pltpu.roll(totals[h], 64, 1)

    def leaf(l, carry):
        near = near_a[l] + near_b[l] + near_c[l]
        leaf_out = (
            far[l] + from_node[pl.ds(pl.multiple_of(l * 8, 8), 8), :]
        )[:, :RANK]
        high, lower = split2(basis[l])
        leaf16 = pieces(leaf_out)
        total = fold(mm(leaf16, high) + mm(leaf16, lower)) + near
        out[l] = fold(mm_nt(pieces(total), one_hot(order[pl.ds(l, 1), :])))
        return carry

    lax.fori_loop(0, LEAVES, leaf, 0, unroll=16)


VM = pl.BlockSpec(memory_space=pltpu.VMEM)
SM = pl.BlockSpec(memory_space=pltpu.SMEM)
ANY = pl.BlockSpec(memory_space=pl.ANY)


HBM = pl.BlockSpec(memory_space=pltpu.HBM)


def near_call(kernel, extra, name, *args):
    return pl.pallas_call(
        kernel,
        out_shape=(jax.ShapeDtypeStruct((LEAVES, PROBES, POINTS), f32), *extra),
        in_specs=[SM, SM] + [VM] * (len(args) - 2),
        out_specs=(VM,) * (1 + len(extra)),
        scratch_shapes=[pltpu.VMEM((LEAVES + 1, 16, POINTS), f32)],
        compiler_params=pltpu.CompilerParams(vmem_limit_bytes=BIG),
        cost_estimate=pl.CostEstimate(
            flops=12 * 10**9, bytes_accessed=30 * 10**6, transcendentals=8 * 10**6
        ),
        name=name,
    )(*args)


def body(
    probes, coords, order, basis, transfer, far_list, far_count, far_coupling, node_list,
    node_count, node_coupling, near_list, near_count,
):
    grp, leaf = lax.axis_index("grp"), lax.axis_index("leaf")
    groups, blocks = lax.axis_size("grp"), lax.axis_size("leaf")
    device = (grp * blocks + leaf).reshape(1).astype(jnp.int32)
    some = lambda *shape: jax.ShapeDtypeStruct(shape, f32)
    ints = lambda *shape: jax.ShapeDtypeStruct(shape, jnp.int32)
    short = lambda *shape: jax.ShapeDtypeStruct(shape, bf16)

    halo, coef, lists, counts, feat, target, s16 = pl.pallas_call(
        up_kernel,
        out_shape=(
            some(LEAVES, 12, POINTS), some(HELD, 4, 128), ints(2, TILE_SLOTS), ints(2),
            short(LEAVES, POINTS, 64), short(LEAVES + 1, 64, POINTS), short(LEAVES, 16, POINTS),
        ),
        in_specs=[SM] + [HBM] * 7,
        out_specs=(VM, VM, SM, SM, VM, VM, VM),
        scratch_shapes=[
            pltpu.VMEM((LEAVES * 8, 128), f32),
            pltpu.VMEM((LEAVES, RANK * RANK), f32),
            pltpu.VMEM((LEAVES, PROBES, POINTS), f32),
            pltpu.VMEM((3, LEAVES, POINTS), f32),
            pltpu.VMEM((LEAVES, POINTS), jnp.int32),
            pltpu.VMEM((LEAVES, RANK, POINTS), f32),
            pltpu.SMEM((8, LEAVES), jnp.int32),
            pltpu.SMEM((LEAVES,), jnp.int32),
            pltpu.SemaphoreType.DMA((LEAVES // CHUNK, 4)),
            pltpu.SemaphoreType.DMA((3,)),
        ],
        compiler_params=pltpu.CompilerParams(vmem_limit_bytes=BIG),
        name="up",
    )(
        device,
        *(
            pltpu.with_memory_space_constraint(array, pltpu.HBM)
            for array in (
                near_list.T, near_count, probes, coords.transpose(1, 0, 2), order, basis, transfer
            )
        ),
    )

    below = lax.ppermute(halo, "leaf", [(i, (i + 1) % blocks) for i in range(blocks)])
    above = lax.ppermute(halo, "leaf", [((i + 1) % blocks, i) for i in range(blocks)])

    def place(y, x, c):
        return ((y % 4) * 4 + x % 4) * 2 + c

    everyone = [(y, x, c) for y in range(4) for x in range(4) for c in range(2)]

    def shift(part, dy, dx, dc):
        pairs = [(place(y + dy, x + dx, c ^ dc), place(y, x, c)) for y, x, c in everyone]
        return lax.ppermute(part, "leaf", pairs)

    along_x = [coef] + [shift(coef, 0, i, 0) for i in range(1, 4)]
    near_a = near_call(near_a_kernel, (), "near_a", lists, counts, feat, target, s16)[0]
    *along_x, near_a, below, above = lax.optimization_barrier((*along_x, near_a, below, above))
    line = jnp.concatenate(along_x, axis=0)
    line, lists_b = lax.optimization_barrier((line, lists))
    planes = [line] + [shift(line, i, 0, 0) for i in range(1, 4)]
    near_b, halo_feat, halo_s16 = near_call(
        near_b_kernel,
        (short(2 * LEAVES, POINTS, 64), short(2 * LEAVES, 16, POINTS)),
        "near_b", lists_b, counts, feat, target, s16, below, above,
    )
    *planes, near_b = lax.optimization_barrier((*planes, near_b))
    own_side = jnp.concatenate(planes, axis=0)
    own_side, lists_c = lax.optimization_barrier((own_side, lists_b))
    other_side = shift(own_side, 0, 0, 1)
    near_c = near_call(
        near_c_kernel, (), "near_c", lists_c, counts, halo_feat, target, halo_s16
    )[0]
    other_side, near_c = lax.optimization_barrier((other_side, near_c))
    nodes = jnp.concatenate(
        [part.reshape(16, HELD, 4, 128)[:, LEAVES] for part in (own_side, other_side)], axis=0
    )
    all_nodes = [nodes] + [
        lax.ppermute(nodes, "grp", [((g + i) % groups, g) for g in range(groups)])
        for i in range(1, groups)
    ]

    lying = far_coupling.reshape(LEAVES, 2, 8, 32, 128).transpose(0, 1, 3, 2, 4).reshape(-1, 128)
    far, node_rows = pl.pallas_call(
        far_kernel,
        out_shape=(some(LEAVES, 8, 128), ints(8)),
        in_specs=[SM, ANY, ANY, ANY, SM, VM, VM, VM],
        out_specs=(VM, SM),
        scratch_shapes=[
            pltpu.VMEM((FAR_CHUNK * 256, 128), f32),
            pltpu.VMEM((LEAVES * 16, 128), bf16),
            pltpu.SMEM((16, LEAVES), jnp.int32),
            pltpu.SMEM((LEAVES,), jnp.int32),
            pltpu.SMEM((1, 8), jnp.int32),
            pltpu.SemaphoreType.DMA((3,)),
        ],
        compiler_params=pltpu.CompilerParams(vmem_limit_bytes=BIG),
        cost_estimate=pl.CostEstimate(
            flops=12 * 10**9, bytes_accessed=20 * 10**6, transcendentals=0
        ),
        name="far",
    )(
        device,
        *(
            pltpu.with_memory_space_constraint(array, pltpu.HBM)
            for array in (far_list.T, far_count, node_list)
        ),
        node_count,
        lying, own_side, other_side,
    )

    return pl.pallas_call(
        down_kernel,
        out_shape=some(LEAVES, PROBES, POINTS),
        in_specs=[SM] + [VM] * 12,
        out_specs=VM,
        scratch_shapes=[
            pltpu.VMEM((129, 4, 128), f32),
            pltpu.VMEM((64, 128), f32),
            pltpu.VMEM((8, RANK * RANK), f32),
            pltpu.VMEM((LEAVES * 8, 128), f32),
        ],
        compiler_params=pltpu.CompilerParams(vmem_limit_bytes=BIG),
        name="down",
    )(
        node_rows, *all_nodes, node_coupling, transfer, basis, order, far, near_a, near_b, near_c
    )


def solution(mesh):
    rows = ("grp", "leaf")
    return jax.shard_map(
        body,
        mesh=mesh,
        in_specs=(
            P(rows, None, None), P(rows, None, None), P(rows, None), P(rows, None, None),
            P(rows, None), P(rows, None), P(rows), P(rows, None, None), P(rows, None), P(rows),
            P(rows, None, None), P(rows, None), P(rows),
        ),
        out_specs=P(rows, None, None),
        check_vma=False,
    )
```
